128 devices in a mesh: leaf: 16 (over z, x), sub: 8 (over y, core).
Axes of the slice: x: 4, y: 4, z: 4, core: 2. Of those that a mesh axis runs over, the one named last changes fastest.
Arguments:
- points: float32 [131072, 64], P(('leaf', 'sub')), may hold values from -6 to 6
- leaf_maps: float32 [256, 128, 512], P(('leaf', 'sub')), may hold values from -0.25 to 0.25
- root_maps: float32 [256, 128, 512], P(('leaf', 'sub')), may hold values from -0.25 to 0.25
- current: float32 [131072], P(('leaf', 'sub')), may hold values from -6 to 6
- krylov_basis: float32 [8, 131072], P(None, ('leaf', 'sub')), may hold values from -0.015625 to 0.015625
- ritz_roots: float32 [2], replicated, may hold values from 40 to 400
- point_order: int32 [131072], P(('leaf', 'sub')), may hold values from 0 to 8191, as said below
- skeleton: int32 [256, 128], P(('leaf', 'sub')), may hold values from 0 to 511, as said below
- root_skeleton: int32 [16, 128], P('leaf'), may hold values from 0 to 8191, as said below
- near_list: int32 [256, 32], P(('leaf', 'sub')), may hold values from 0 to 47, as said below
- far_list: int32 [256, 4], P(('leaf', 'sub')), may hold values from 0 to 47, as said below
Outputs:
- orthogonal: float32 [131072], P(('leaf', 'sub'))
- hessenberg: float32 [9], replicated
The draws below stay inside these ranges and needn't reach their ends.
Inputs may be any that keep to these rules, and one draw needn't show every extreme that they name: Within each subtree (block of 8192 tree positions) point_order is a permutation of 0 to 8191. `skeleton`: each row holds 128 different point numbers of the leaf. `root_skeleton`: each row holds 128 different point numbers of the subtree. `near_list`: slots count 16 leaves of the previous subtree, then the own subtree, then the next one (circularly). The first slot of leaf a is its own, 16 + (a mod 16); the slots of a row are different, and no slot of a row is in the leaf's far_list. `far_list`: slots as in near_list; different within a row, never the leaf's own.
All inputs are finite; a program needn't handle non-finite values.
Results may differ from the reference program's by a relative error of at most 0.000096.
Values sent between devices are 32-bit elements; how exact they have to be, the bound alone decides.
No kernel may reach another device: no remote copies, remote signals or barrier semaphores. Data moves between devices by JAX's collectives and lax.ppermute only.
A program may use at most 64 MiB of HBM per device.

```python
import math
import jax
import jax.numpy as jnp
from jax import lax

F = 64
LS = 512
SK = 128
NEAR = 32
FAR = 4
MB = 8
SUBLEAVES = 16
SUBTREES = 16
LEAVES = 256
NPTS = 131072


def slot_tables(key):
    base = jax.random.fold_in(key, 11)
    keys = jax.random.split(base, LEAVES)
    others = jax.vmap(lambda leafkey: jax.random.permutation(leafkey, 3 * SUBLEAVES - 1))(keys).astype(jnp.int32)
    own_slot = (SUBLEAVES + jnp.arange(LEAVES, dtype=jnp.int32) % SUBLEAVES)[:, None].astype(jnp.int32)
    shifted = jnp.where(others >= own_slot, others + 1, others).astype(jnp.int32)
    return (own_slot, shifted)


def draw_near_list(key, part):
    own_slot, shifted = slot_tables(key)
    return jnp.concatenate([own_slot, shifted[:, :NEAR - 1]], axis=1).astype(jnp.int32)


def draw_far_list(key, part):
    own_slot, shifted = slot_tables(key)
    return shifted[:, NEAR - 1:NEAR - 1 + FAR].astype(jnp.int32)


def draw_point_order(key, part):
    keys = jax.random.split(jax.random.fold_in(key, 23), SUBTREES)
    table = jax.vmap(lambda subkey: jax.random.permutation(subkey, SUBLEAVES * LS))(keys)
    return table.reshape(-1).astype(jnp.int32)


def draw_skeleton(key, part):
    keys = jax.random.split(jax.random.fold_in(key, 37), LEAVES)
    table = jax.vmap(lambda leafkey: jax.random.permutation(leafkey, LS)[:SK])(keys)
    return table.astype(jnp.int32)


def draw_root_skeleton(key, part):
    keys = jax.random.split(jax.random.fold_in(key, 41), SUBTREES)
    table = jax.vmap(lambda subkey: jax.random.permutation(subkey, SUBLEAVES * LS)[:SK])(keys)
    return table.astype(jnp.int32)


def levels(stream_key, dims, pieces, smallest, high):
    def one(axis_at, parts):
        heights = jax.random.uniform(jax.random.fold_in(jax.random.fold_in(stream_key, 6), axis_at), (parts,), jnp.float32, smallest / len(pieces), high / len(pieces))
        return jnp.repeat(jnp.exp(heights), dims[axis_at] // parts).reshape((-1,) + (1,) * (len(dims) - axis_at - 1))

    loudness = one(*pieces[0])
    for cut in pieces[1:]:
        loudness = loudness * one(*cut)
    return loudness


def scatter_about(own_key, extent, width, bound, shards=(), kind=jnp.bfloat16):
    values = width * jax.random.normal(own_key, extent, jnp.float32)
    if shards:
        values = values * levels(own_key, extent, shards, -0.22, 0.18)
    return jnp.clip(values, -bound, bound).astype(kind)


def setup_inputs(seed: int = 0) -> dict:
    streams_of = jax.random.split(jax.random.key(seed), 12)
    return {
        "points": scatter_about(streams_of[0], (NPTS, F), 1.0, 6.0, ((0, 128),), jnp.float32),
        "leaf_maps": scatter_about(streams_of[1], (LEAVES, SK, LS), LS ** -0.5, 0.25, ((0, 128),), jnp.float32),
        "root_maps": scatter_about(streams_of[2], (LEAVES, SK, LS), LS ** -0.5, 0.25, ((0, 128),), jnp.float32),
        "current": scatter_about(streams_of[3], (NPTS,), 1.0, 6.0, ((0, 128),), jnp.float32),
        "krylov_basis": scatter_about(streams_of[4], (MB, NPTS), NPTS ** -0.5, 0.015625, ((1, 128),), jnp.float32),
        "ritz_roots": jnp.clip(jnp.exp(jax.random.uniform(streams_of[5], (2,), jnp.float32, math.log(40.0), math.log(400.0))), 40.0, 400.0),
        "point_order": draw_point_order(jax.random.fold_in(streams_of[11], 71), 0),
        "skeleton": draw_skeleton(jax.random.fold_in(streams_of[11], 71), 0),
        "root_skeleton": draw_root_skeleton(jax.random.fold_in(streams_of[11], 71), 0),
        "near_list": draw_near_list(jax.random.fold_in(streams_of[11], 71), 0),
        "far_list": draw_far_list(jax.random.fold_in(streams_of[11], 71), 0),
    }


HIGHEST_PREC = lax.Precision.HIGHEST
RIDGE_SHIFT = 1.0
EPSILON = 1e-06

def gaussian(inner_prod, target_sq, source_sq, feat_count):
    return jnp.exp(-(target_sq + source_sq - 2.0 * inner_prod) / feat_count)

def reference(points, leaf_maps, root_maps, current, krylov_basis, ritz_roots, point_order, skeleton, root_skeleton, near_list, far_list):
    feat_count = points.shape[1]
    leaf_points = points.reshape(LEAVES, LS, F)
    leaf_sq = lax.optimization_barrier(jnp.sum(leaf_points * leaf_points, axis=-1))
    skel_points = jnp.take_along_axis(leaf_points, skeleton[:, :, None], axis=1)
    skel_sq = lax.optimization_barrier(jnp.sum(skel_points * skel_points, axis=-1))
    subtree_of = (jnp.arange(LEAVES, dtype=jnp.int32) // SUBLEAVES).astype(jnp.int32)

    def to_global(window_slots):
        offset = window_slots // SUBLEAVES - 1
        return ((subtree_of[:, None] + offset) % SUBTREES * SUBLEAVES + window_slots % SUBLEAVES).astype(jnp.int32)
    near_global = to_global(near_list)
    far_global = to_global(far_list)
    far_points = skel_points[far_global]
    far_inner = jnp.einsum('bmf,bjnf->bjmn', skel_points, far_points, precision=HIGHEST_PREC)
    far_kernel = gaussian(far_inner, skel_sq[:, None, :, None], skel_sq[far_global][:, :, None, :], feat_count)
    subtree_points = points.reshape(SUBTREES, SUBLEAVES * LS, F)
    root_points = jnp.take_along_axis(subtree_points, root_skeleton[:, :, None], axis=1).reshape(SUBTREES * SK, F)
    root_sq = lax.optimization_barrier(jnp.sum(root_points * root_points, axis=-1))
    root_inner = jnp.dot(root_points, root_points.T, precision=HIGHEST_PREC)
    top_kernel = gaussian(root_inner, root_sq[:, None], root_sq[None, :], feat_count)
    distance = (jnp.arange(SUBTREES)[None, :] - jnp.arange(SUBTREES)[:, None]) % SUBTREES
    far_mask = (distance >= 1).astype(jnp.float32)
    top_kernel = top_kernel * jnp.repeat(jnp.repeat(far_mask, SK, axis=0), SK, axis=1)

    def operator(vector):
        values = vector.reshape(LEAVES, LS)
        skel_weights = jnp.einsum('bkn,bn->bk', leaf_maps, values, precision=HIGHEST_PREC)
        root_weights = jnp.einsum('bkn,bn->bk', root_maps, values, precision=HIGHEST_PREC).reshape(SUBTREES, SUBLEAVES, SK).sum(axis=1)

        def near_one(packed):
            targets, target_sq, neighbours = packed
            sources = leaf_points[neighbours]
            inner_prod = jnp.einsum('mf,jnf->jmn', targets, sources, precision=HIGHEST_PREC)
            kernel = gaussian(inner_prod, target_sq[None, :, None], leaf_sq[neighbours][:, None, :], feat_count)
            return jnp.einsum('jmn,jn->m', kernel, values[neighbours], precision=HIGHEST_PREC)
        result = lax.map(near_one, (leaf_points, leaf_sq, near_global))
        skel_out = jnp.einsum('bjmn,bjn->bm', far_kernel, skel_weights[far_global], precision=HIGHEST_PREC)
        result = result + jnp.einsum('bkn,bk->bn', leaf_maps, skel_out, precision=HIGHEST_PREC)
        root_out = jnp.dot(top_kernel, root_weights.reshape(-1), precision=HIGHEST_PREC).reshape(SUBTREES, SK)
        result = result + jnp.einsum('bkn,bk->bn', root_maps, root_out[subtree_of], precision=HIGHEST_PREC)
        return result.reshape(-1) + RIDGE_SHIFT * vector
    order_rows = point_order.reshape(SUBTREES, SUBLEAVES * LS)
    tree_vector = jnp.take_along_axis(current.reshape(SUBTREES, SUBLEAVES * LS), order_rows, axis=1).reshape(-1)
    first_section = tree_vector - operator(tree_vector) / ritz_roots[0]
    second = first_section - operator(first_section) / ritz_roots[1]
    preconditioned = (tree_vector - second).reshape(SUBTREES, SUBLEAVES * LS)
    user_grown = jax.vmap(lambda positions, entries: jnp.zeros_like(entries).at[positions].set(entries))(order_rows, preconditioned).reshape(-1)
    projections = jnp.dot(krylov_basis, user_grown, precision=HIGHEST_PREC)
    orthogonal = user_grown - jnp.dot(projections, krylov_basis, precision=HIGHEST_PREC)
    length_norm = jnp.sqrt(jnp.sum(orthogonal * orthogonal) + EPSILON)
    return (orthogonal, jnp.concatenate([projections, length_norm[None]]))
```

```python
import functools
import math

import jax
import jax.numpy as jnp
from jax import lax
from jax.experimental import pallas as pl
from jax.experimental.pallas import tpu as pltpu
from jax.sharding import PartitionSpec as P

F32 = jnp.float32
BF16 = jnp.bfloat16
HI = lax.Precision.HIGHEST
RIDGE = 1.0
EPSILON = 1e-06
LANES = 128
BOTH = ("leaf", "sub")
VMEM_LIMIT = 50 * 1024 * 1024
NT = (((1,), (1,)), ((), ()))
TN = (((0,), (0,)), ((), ()))


def dot(a, b, dims=(((1,), (0,)), ((), ())), precision=None):
    return lax.dot_general(a, b, dims, precision=precision, preferred_element_type=F32)


def halves(x):
    h = x.astype(BF16)
    return h, (x - h.astype(F32)).astype(BF16)


def thirds(x):
    a = x.astype(BF16)
    r = x - a.astype(F32)
    b = r.astype(BF16)
    return a, b, (r - b.astype(F32)).astype(BF16)


def row_sums(block):
    return dot(jnp.ones((8, LANES), F32), block, NT, HI)[:1]


def half_norm(h, l):
    x = h.astype(F32) + l.astype(F32)
    return jnp.exp2(-0.5 * jnp.sum(x * x, axis=0, keepdims=True))


def pick(index_row, count):
    shape = (count, index_row.shape[1])
    return lax.broadcasted_iota(jnp.int32, shape, 0) == jnp.broadcast_to(index_row, shape)


def split_order(order):
    row = (lax.shift_right_logical(order, 7) & 7) * 8 + lax.shift_right_logical(order, 10)
    return row, order & 127


def call(body, outs, *args, smem=(), scratch=(), cost=None, name=None):
    specs = [
        pl.BlockSpec(memory_space=pltpu.SMEM if i in smem else pltpu.VMEM) for i in range(len(args))
    ]
    return pl.pallas_call(
        body,
        out_shape=outs,
        in_specs=specs,
        out_specs=[pl.BlockSpec(memory_space=pltpu.VMEM)] * len(outs),
        scratch_shapes=list(scratch),
        compiler_params=pltpu.CompilerParams(vmem_limit_bytes=VMEM_LIMIT),
        cost_estimate=cost,
        name=name,
    )(*args)


def prepare_kernel(
    scale, leaf_size, pts, qt, skel, rskel, cur, basis, lhs, u_row, z_lhs, uz_row, sent, gram
):
    per_device = skel.shape[0]
    feats, count = qt.shape
    ph, pl_ = halves(pts[...] * scale)
    lhs[...] = jnp.concatenate([ph, pl_, ph, pl_], axis=1)
    qh, ql = halves(qt[...])
    u_row[...] = half_norm(qh, ql)
    both = jnp.concatenate([qh, ql], axis=0)
    for a in range(per_device):
        hot = pick(skel[a : a + 1, :], leaf_size).astype(F32).astype(BF16)
        z = dot(both[:, a * leaf_size : (a + 1) * leaf_size], hot).astype(BF16)
        zh, zl = z[:feats], z[feats:]
        z_lhs[a] = jnp.concatenate([zh, zl, zh, zl], axis=0)
        uz_row[a : a + 1, :] = half_norm(zh, zl)
    hot = pick(rskel[...], count).astype(F32).astype(BF16)
    r = dot(both, hot)
    r = r[:feats] + r[feats:]
    subs = sent.shape[0]
    sent[:, :count] = jnp.broadcast_to(cur[...], (subs, count))
    for f in range(feats // subs):
        sent[:, count + f * LANES : count + (f + 1) * LANES] = r[f * subs : (f + 1) * subs]
    g = dot(basis[...], basis[...], NT, HI)
    vecs = basis.shape[0]
    lane = lax.broadcasted_iota(jnp.int32, (vecs, LANES), 1)
    sub = lax.broadcasted_iota(jnp.int32, (vecs, LANES), 0)
    wide = dot(g, ((lane & (vecs - 1)) == sub).astype(F32), precision=HI)
    gram[...] = jnp.sum(jnp.where(lane // vecs == sub, wide, 0.0), axis=0, keepdims=True)


def weights(v, lm, rm):
    per_device, _, leaf_size = lm.shape
    root = None
    skel = []
    for a in range(per_device):
        piece = jnp.broadcast_to(v[:, a * leaf_size : (a + 1) * leaf_size], (8, leaf_size))
        skel.append(dot(piece, lm[a], NT, HI)[:1])
        part = dot(piece, rm[a], NT, HI)[:1]
        root = part if root is None else root + part
    return skel, root


def packed_vector(v, u_row, uz_row, lm, rm):
    skel, root = weights(v, lm, rm)
    scaled = [skel[a] * uz_row[a : a + 1, :] for a in range(len(skel))]
    return [v * u_row[...]] + scaled + [root]


def start_kernel(got, order, u_row, uz_row, lm, rm, skel, gram, v_row, sent):
    subs = got.shape[0]
    count = order.shape[1]
    tiles = count // LANES
    cur = jnp.concatenate([got[:, k * LANES : (k + 1) * LANES] for k in range(tiles)], axis=0)
    row, lane = split_order(order[...])
    hot = pick(row, subs * tiles).astype(F32).astype(BF16)
    picked = sum(dot(part, hot, TN) for part in thirds(cur))
    v = jnp.sum(jnp.where(pick(lane, LANES), picked, 0.0), axis=0, keepdims=True)
    v_row[...] = v
    sums = []
    for k in range(tiles):
        at = count + k * LANES
        sums.append(jnp.sum(got[:, at : at + LANES], axis=0, keepdims=True))
    skels = [skel[a : a + 1, :].astype(F32) for a in range(skel.shape[0])]
    block = jnp.concatenate(
        packed_vector(v, u_row, uz_row, lm, rm) + skels + sums + [gram[...]], axis=1
    )
    sent[...] = jnp.broadcast_to(block, sent.shape)


def apply_operator(
    info, window, lhs, z_lhs, u_row, uz_row, lm, rm, v_row, vec, tab, acc, far_acc, rhs
):
    per_device, skel_count, leaf_size = lm.shape
    subs, sides, feats, count = window.shape
    skel_at = count + per_device * skel_count
    tab_skel = skel_at + skel_count
    tab_root = tab_skel + per_device * skel_count
    leaf_count = vec.shape[0] // subs
    me = info[2 * per_device, 0]
    acc[...] = jnp.zeros_like(acc)
    far_acc[...] = jnp.zeros_like(far_acc)
    step_rows = 128

    def chunk(i, carry):
        side = i // subs
        dev = i % subs
        owner = (me + side + leaf_count - 1) % leaf_count
        rows = pl.ds(pl.multiple_of(owner * subs, subs), subs)

        def row_of(ref, at, size):
            block = ref[rows, at : at + size]
            mine = lax.broadcasted_iota(jnp.int32, block.shape, 0) == dev
            return jnp.sum(jnp.where(mine, block, 0.0), axis=0, keepdims=True)

        for j in range(per_device):
            slot = i * per_device + j
            qh, ql = halves(window[dev, side, :, j * leaf_size : (j + 1) * leaf_size])
            rhs[0 * feats : 1 * feats, :] = qh
            rhs[1 * feats : 2 * feats, :] = qh
            rhs[2 * feats : 3 * feats, :] = ql
            rhs[3 * feats : 4 * feats, :] = ql
            for a in range(per_device):

                @pl.when(info[a, slot] > 0)
                def near():
                    w = row_of(vec, j * leaf_size, leaf_size)
                    for r in range(leaf_size // step_rows):
                        at = a * leaf_size + r * step_rows
                        e = jnp.exp2(dot(lhs[at : at + step_rows, :], rhs[...]))
                        total = acc[at : at + step_rows, :]
                        for k in range(leaf_size // LANES):
                            part = slice(k * LANES, (k + 1) * LANES)
                            total = total + e[:, part] * w[:, part]
                        acc[at : at + step_rows, :] = total

            for a in range(per_device):

                @pl.when(info[per_device + a, slot] > 0)
                def far():
                    at = tab_skel + j * skel_count
                    index = row_of(tab, at, skel_count).astype(jnp.int32)
                    hot = pick(index, leaf_size).astype(F32).astype(BF16)
                    z = dot(rhs[feats : 3 * feats, :], hot).astype(BF16)
                    zh, zl = z[:feats], z[feats:]
                    z4 = jnp.concatenate([zh, zh, zl, zl], axis=0)
                    e = jnp.exp2(dot(z_lhs[a], z4, TN))
                    at = count + j * skel_count
                    w = row_of(vec, at, skel_count)
                    far_acc[a * skel_count : (a + 1) * skel_count, :] += e * w

        return carry

    lax.fori_loop(0, sides * subs, chunk, 0)

    def root_points(u):
        rows = pl.ds(pl.multiple_of(u * subs, subs), subs)
        r = jnp.concatenate(
            [
                tab[rows, tab_root + f * skel_count : tab_root + (f + 1) * skel_count]
                for f in range(feats // subs)
            ],
            axis=0,
        )
        return halves(r)

    rh, rl = root_points(me)
    r_lhs = jnp.concatenate([rh, rl, rh, rl], axis=0)
    own_norm = half_norm(rh, rl)

    def subtree(u, total):
        h, l = root_points(u)
        e = jnp.exp2(dot(r_lhs, jnp.concatenate([h, h, l, l], axis=0), TN))
        rows = pl.ds(pl.multiple_of(u * subs, subs), subs)
        w = jnp.sum(vec[rows, skel_at : skel_at + skel_count], axis=0, keepdims=True)
        w = jnp.where(u == me, 0.0, w * half_norm(h, l))
        return total + e * w

    top = lax.fori_loop(0, leaf_count, subtree, jnp.zeros((skel_count, skel_count), F32))
    root_out = jnp.broadcast_to(row_sums(top) * own_norm, (8, skel_count))
    outs = []
    for a in range(per_device):
        part = slice(a * leaf_size, (a + 1) * leaf_size)
        y = row_sums(acc[part, :]) * u_row[:, part]
        skel_out = row_sums(far_acc[a * skel_count : (a + 1) * skel_count, :]) * uz_row[a : a + 1, :]
        y = y + dot(jnp.broadcast_to(skel_out, (8, skel_count)), lm[a], precision=HI)[:1]
        y = y + dot(root_out, rm[a], precision=HI)[:1]
        outs.append(y + RIDGE * v_row[:, part])
    return jnp.concatenate(outs, axis=1)


def first_kernel(
    info, ritz, window, lhs, z_lhs, u_row, uz_row, lm, rm, v_row, vec, first_row, sent, acc, far_acc, rhs
):
    y = apply_operator(
        info, window, lhs, z_lhs, u_row, uz_row, lm, rm, v_row, vec, vec, acc, far_acc, rhs
    )
    first = v_row[...] - y / ritz[0]
    first_row[...] = first
    block = jnp.concatenate(packed_vector(first, u_row, uz_row, lm, rm), axis=1)
    sent[...] = jnp.broadcast_to(block, sent.shape)


def second_kernel(
    info, ritz, window, lhs, z_lhs, u_row, uz_row, lm, rm, v_row, vec, tab, tree_row, order, sent, acc, far_acc, rhs
):
    y = apply_operator(
        info, window, lhs, z_lhs, u_row, uz_row, lm, rm, v_row, vec, tab, acc, far_acc, rhs
    )
    grown = tree_row[...] - (v_row[...] - y / ritz[1])
    subs, count = sent.shape
    tiles = count // LANES
    row, lane = split_order(order[...])
    spread = jnp.where(pick(row, subs * tiles), grown, 0.0)
    hot = pick(lane, LANES).astype(F32).astype(BF16)
    placed = sum(dot(part, hot, NT) for part in thirds(spread))
    for k in range(tiles):
        sent[:, k * LANES : (k + 1) * LANES] = placed[k * subs : (k + 1) * subs]


def project_kernel(got, basis, user_row, sent):
    user = jnp.sum(got[...], axis=0, keepdims=True)
    user_row[...] = user
    b = basis[...]
    vecs = b.shape[0]
    proj = jnp.sum(b * user, axis=1, keepdims=True)
    norm = jnp.sum(user * user, axis=1, keepdims=True)
    lane = lax.broadcasted_iota(jnp.int32, (vecs, LANES), 1)
    sub = lax.broadcasted_iota(jnp.int32, (vecs, LANES), 0)
    row = jnp.sum(jnp.where(lane == sub, proj, 0.0), axis=0, keepdims=True)
    row = row + jnp.where(lane[:1] == vecs, norm, 0.0)
    sent[...] = jnp.broadcast_to(row, sent.shape)


def finish_kernel(got, tab, basis, user_row, orth, hess):
    b = basis[...]
    vecs = b.shape[0]
    total = jnp.sum(got[...], axis=0, keepdims=True)
    width = tab.shape[1]
    gram = jnp.sum(tab[:, width - LANES :], axis=0, keepdims=True)
    lane = lax.broadcasted_iota(jnp.int32, (vecs, LANES), 1)
    sub = lax.broadcasted_iota(jnp.int32, (vecs, LANES), 0)
    proj = jnp.sum(jnp.where(lane == sub, total, 0.0), axis=1, keepdims=True)
    left = jnp.sum(jnp.where(lane // vecs == sub, proj, 0.0), axis=0, keepdims=True)
    right = jnp.sum(jnp.where((lane & (vecs - 1)) == sub, proj, 0.0), axis=0, keepdims=True)
    one = lane[:1]
    norm = jnp.sum(jnp.where(one == vecs, total, 0.0), axis=1, keepdims=True)
    cross = jnp.sum(jnp.where(one < vecs, total * total, 0.0), axis=1, keepdims=True)
    quad = jnp.sum(left * right * gram, axis=1, keepdims=True)
    length = jnp.sqrt(jnp.maximum(norm - 2.0 * cross + quad, 0.0) + EPSILON)
    orth[...] = user_row[...] - jnp.sum(proj * b, axis=0, keepdims=True)
    hess[...] = jnp.where(one < vecs, total, jnp.broadcast_to(length, (1, LANES)))


def shards(
    points,
    leaf_maps,
    root_maps,
    current,
    krylov_basis,
    ritz_roots,
    point_order,
    skeleton,
    root_skeleton,
    near_list,
    far_list,
):
    per_device, skel_count, leaf_size = leaf_maps.shape
    count, feats = points.shape
    vecs = krylov_basis.shape[0]
    subs = lax.axis_size("sub")
    leaves = lax.axis_size("leaf")
    everyone = subs * leaves
    me = lax.axis_index("leaf")
    scale = math.sqrt(math.log2(math.e) / (feats / 2.0))
    qt = points.T * F32(scale)
    ring = [(i, (i + 1) % leaves) for i in range(leaves)]
    back = [(j, i) for i, j in ring]
    low = lax.ppermute(qt, "leaf", ring)
    high = lax.ppermute(qt, "leaf", back)
    window = lax.all_gather(jnp.stack([low, qt, high]), "sub", axis=0)

    sds = jax.ShapeDtypeStruct
    slots = jnp.arange(3 * subs * per_device, dtype=jnp.int32)
    near = jnp.any(near_list[:, :, None] == slots, axis=1).astype(jnp.int32)
    far = jnp.any(far_list[:, :, None] == slots, axis=1).astype(jnp.int32)
    info = jnp.concatenate([near, far, jnp.full((1, slots.shape[0]), me, jnp.int32)], axis=0)
    order = point_order.reshape(1, count)
    rskel = root_skeleton - lax.axis_index("sub") * count

    lhs, u_row, z_lhs, uz_row, sent, gram = call(
        functools.partial(prepare_kernel, scale, leaf_size),
        [
            sds((count, 4 * feats), BF16),
            sds((1, count), F32),
            sds((per_device, 4 * feats, skel_count), BF16),
            sds((per_device, skel_count), F32),
            sds((subs, count + (feats // subs) * skel_count), F32),
            sds((1, LANES), F32),
        ],
        points,
        qt,
        skeleton,
        rskel,
        current.reshape(1, count),
        krylov_basis,
        name="prepare",
    )
    got = lax.all_to_all(sent, "sub", 0, 0, tiled=True)
    vec_width = count + per_device * skel_count + skel_count
    tab_width = vec_width + per_device * skel_count + (feats // subs) * skel_count + LANES
    tree_row, sent = call(
        start_kernel,
        [sds((1, count), F32), sds((everyone, tab_width), F32)],
        got,
        order,
        u_row,
        uz_row,
        leaf_maps,
        root_maps,
        skeleton,
        gram,
        name="start",
    )
    tab = lax.all_to_all(sent, BOTH, 0, 0, tiled=True)
    scratch = [
        pltpu.VMEM((count, LANES), F32),
        pltpu.VMEM((per_device * skel_count, skel_count), F32),
        pltpu.VMEM((4 * feats, leaf_size), BF16),
    ]
    shared = (info, ritz_roots, window, lhs, z_lhs, u_row, uz_row, leaf_maps, root_maps)
    first_row, sent = call(
        first_kernel,
        [sds((1, count), F32), sds((everyone, vec_width), F32)],
        *shared,
        tree_row,
        tab,
        smem=(0, 1),
        scratch=scratch,
        name="first",
    )
    vec = lax.all_to_all(sent, BOTH, 0, 0, tiled=True)
    (sent,) = call(
        second_kernel,
        [sds((subs, count), F32)],
        *shared,
        first_row,
        vec,
        tab,
        tree_row,
        order,
        smem=(0, 1),
        scratch=scratch,
        name="second",
    )
    got = lax.all_to_all(sent, "sub", 0, 0, tiled=True)
    user_row, sent = call(
        project_kernel,
        [sds((1, count), F32), sds((everyone, LANES), F32)],
        got,
        krylov_basis,
        name="project",
    )
    got = lax.all_to_all(sent, BOTH, 0, 0, tiled=True)
    orth, hess = call(
        finish_kernel,
        [sds((1, count), F32), sds((1, LANES), F32)],
        got,
        tab,
        krylov_basis,
        user_row,
        name="finish",
    )
    return orth.reshape(count), hess[0, : vecs + 1]


def solution(mesh):
    return jax.shard_map(
        shards,
        mesh=mesh,
        in_specs=(
            P(("leaf", "sub"), None),
            P(("leaf", "sub"), None, None),
            P(("leaf", "sub"), None, None),
            P(("leaf", "sub")),
            P(None, ("leaf", "sub")),
            P(),
            P(("leaf", "sub")),
            P(("leaf", "sub"), None),
            P("leaf", None),
            P(("leaf", "sub"), None),
            P(("leaf", "sub"), None),
        ),
        out_specs=(P(("leaf", "sub")), P()),
        check_vma=False,
    )
```

```python
import functools
import math

import jax
import jax.numpy as jnp
from jax import lax
from jax.experimental import pallas as pl
from jax.experimental.pallas import tpu as pltpu
from jax.sharding import PartitionSpec as P

F32 = jnp.float32
BF16 = jnp.bfloat16
HI = lax.Precision.HIGHEST
RIDGE = 1.0
EPSILON = 1e-06
LANES = 128
BOTH = ("leaf", "sub")
STEP = 256
UNROLL = 8
VMEM_LIMIT = 50 * 1024 * 1024
NT = (((1,), (1,)), ((), ()))
TN = (((0,), (0,)), ((), ()))


def dot(a, b, dims=(((1,), (0,)), ((), ())), precision=None):
    return lax.dot_general(a, b, dims, precision=precision, preferred_element_type=F32)


def halves(x):
    h = x.astype(BF16)
    return h, (x - h.astype(F32)).astype(BF16)


def thirds(x):
    a = x.astype(BF16)
    r = x - a.astype(F32)
    b = r.astype(BF16)
    return a, b, (r - b.astype(F32)).astype(BF16)


def row_sums(block):
    return jnp.sum(block.T, axis=0, keepdims=True)


def fold(wide):
    return sum(wide[:, at : at + LANES] for at in range(0, wide.shape[1], LANES))


def half_norm(h, l):
    x = h.astype(F32) + l.astype(F32)
    return jnp.exp2(-0.5 * jnp.sum(x * x, axis=0, keepdims=True))


def pick(index_row, count):
    shape = (count, index_row.shape[1])
    return lax.broadcasted_iota(jnp.int32, shape, 0) == jnp.broadcast_to(index_row, shape)


def split_order(order):
    row = (lax.shift_right_logical(order, 7) & 7) * 8 + lax.shift_right_logical(order, 10)
    return row, order & 127


def call(body, outs, *args, smem=(), far=(), scratch=(), cost=None, name=None):
    places = [pltpu.SMEM if i in smem else pl.ANY if i in far else pltpu.VMEM for i in range(len(args))]
    specs = [pl.BlockSpec(memory_space=place) for place in places]
    return pl.pallas_call(
        body,
        out_shape=outs,
        in_specs=specs,
        out_specs=[pl.BlockSpec(memory_space=pltpu.VMEM)] * len(outs),
        scratch_shapes=list(scratch),
        compiler_params=pltpu.CompilerParams(vmem_limit_bytes=VMEM_LIMIT),
        cost_estimate=cost,
        name=name,
    )(*args)


def prepare_kernel(
    scale, leaf_size, pts, qt, skel, rskel, cur, basis, lhs, u_row, z_lhs, uz_row, uz_col, sent, gram
):
    per_device, skel_count = skel.shape
    feats, count = qt.shape
    ph, pl_ = halves(pts[...] * scale)
    lhs[...] = jnp.concatenate([ph, pl_, ph, pl_], axis=1)
    qh, ql = halves(qt[...])
    u_row[...] = half_norm(qh, ql)
    both = jnp.concatenate([qh, ql], axis=0)
    for a in range(per_device):
        hot = pick(skel[a : a + 1, :], leaf_size).astype(F32).astype(BF16)
        z = dot(both[:, a * leaf_size : (a + 1) * leaf_size], hot)
        zh, zl = z[:feats].astype(BF16), z[feats:].astype(BF16)
        uz_row[a : a + 1, :] = half_norm(zh, zl)
        turned = z.T
        out = slice(a * skel_count, (a + 1) * skel_count)
        z_lhs[out, :] = jnp.concatenate([turned, turned], axis=1).astype(BF16)
        whole = turned[:, :feats] + turned[:, feats:]
        norm = jnp.exp2(-0.5 * jnp.sum(whole * whole, axis=1, keepdims=True))
        uz_col[out, :] = jnp.broadcast_to(norm, (skel_count, LANES))
    hot = pick(rskel[...], count).astype(F32).astype(BF16)
    r = dot(both, hot)
    r = r[:feats] + r[feats:]
    subs = sent.shape[0]
    sent[:, :count] = jnp.broadcast_to(cur[...], (subs, count))
    for f in range(feats // subs):
        sent[:, count + f * LANES : count + (f + 1) * LANES] = r[f * subs : (f + 1) * subs]
    g = dot(basis[...], basis[...], NT, HI)
    vecs = basis.shape[0]
    lane = lax.broadcasted_iota(jnp.int32, (vecs, LANES), 1)
    sub = lax.broadcasted_iota(jnp.int32, (vecs, LANES), 0)
    wide = dot(g, ((lane & (vecs - 1)) == sub).astype(F32), precision=HI)
    gram[...] = jnp.sum(jnp.where(lane // vecs == sub, wide, 0.0), axis=0, keepdims=True)


def packed_vector(v, u_row, uz_row, lm, rm):
    per_device, _, leaf_size = lm.shape
    root = None
    skel = []
    for a in range(per_device):
        piece = v[:, a * leaf_size : (a + 1) * leaf_size]
        skel.append(row_sums(fold(lm[a] * piece)) * uz_row[a : a + 1, :])
        part = fold(rm[a] * piece)
        root = part if root is None else root + part
    return [v * u_row[...]] + skel + [row_sums(root)]


def start_kernel(got, order, u_row, uz_row, lm, rm, skel, gram, v_row, sent):
    subs = got.shape[0]
    count = order.shape[1]
    tiles = count // LANES
    cur = jnp.concatenate([got[:, k * LANES : (k + 1) * LANES] for k in range(tiles)], axis=0)
    row, lane = split_order(order[...])
    hot = pick(row, subs * tiles).astype(F32).astype(BF16)
    picked = sum(dot(part, hot, TN) for part in thirds(cur))
    v = jnp.sum(jnp.where(pick(lane, LANES), picked, 0.0), axis=0, keepdims=True)
    v_row[...] = v
    sums = []
    for k in range(tiles):
        at = count + k * LANES
        sums.append(jnp.sum(got[:, at : at + LANES], axis=0, keepdims=True))
    skels = [skel[a : a + 1, :].astype(F32) for a in range(skel.shape[0])]
    block = jnp.concatenate(
        packed_vector(v, u_row, uz_row, lm, rm) + skels + sums + [gram[...]], axis=1
    )
    sent[...] = jnp.broadcast_to(block, sent.shape)


def top_kernel(feats, info, tab, blocks):
    leaf_count, skel_count, _ = blocks.shape
    subs = tab.shape[0] // leaf_count
    at = tab.shape[1] - LANES - feats // subs * skel_count
    me = info[info.shape[0] - 1, 0]

    def root_points(u):
        rows = pl.ds(pl.multiple_of(u * subs, subs), subs)
        tiles = [tab[rows, at + f * skel_count : at + (f + 1) * skel_count] for f in range(feats // subs)]
        return jnp.concatenate(tiles, axis=0)

    turned = root_points(me).T
    th, tl = halves(turned)
    left = jnp.concatenate([th, tl, th, tl], axis=1)
    whole = th.astype(F32) + tl.astype(F32)
    own = jnp.exp2(-0.5 * jnp.sum(whole * whole, axis=1, keepdims=True))

    def subtree(u, carry):
        h, l = halves(root_points(u))
        e = jnp.exp2(dot(left, jnp.concatenate([h, h, l, l], axis=0)))
        side = jnp.where(u == me, 0.0, half_norm(h, l))
        blocks[u] = e * side * own
        return carry

    lax.fori_loop(0, leaf_count, subtree, 0, unroll=2)


def owners(info, leaf_count, sides):
    me = info[info.shape[0] - 1, 0]
    return [(me + side + leaf_count - 1) % leaf_count for side in range(sides)]


def spread_values(info, vec, values, subs, leaf_size):
    slots = values.shape[0]
    leaf_count = vec.shape[0] // subs
    per_side = slots // 3
    for side, owner in enumerate(owners(info, leaf_count, 3)):
        block = vec[pl.ds(pl.multiple_of(owner * subs, subs), subs), : per_side // subs * leaf_size]
        for n in range(per_side):
            dev, j = n // (per_side // subs), n % (per_side // subs)
            row = block[dev : dev + 1, j * leaf_size : (j + 1) * leaf_size]
            values[side * per_side + n] = jnp.broadcast_to(row, (8, leaf_size))


def picked_row(ref, info, slot, per_side, subs, offset, size):
    leaf_count = ref.shape[0] // subs
    me = info[info.shape[0] - 1, 0]
    per_device = per_side // subs
    side, n = slot // per_side, slot % per_side
    owner = (me + side + leaf_count - 1) % leaf_count
    rows = pl.ds(pl.multiple_of(owner * subs, subs), subs)
    block = ref[rows, offset : offset + per_device * size]
    sub = lax.broadcasted_iota(jnp.int32, (subs, size), 0)
    out = jnp.zeros((1, size), F32)
    for j in range(per_device):
        mine = (sub == n // per_device) & (n % per_device == j)
        part = block[:, j * size : (j + 1) * size]
        out = out + jnp.sum(jnp.where(mine, part, 0.0), axis=0, keepdims=True)
    return out


def quad(pair):
    feats = pair.shape[0] // 2
    h, l = pair[:feats, :], pair[feats:, :]
    return jnp.concatenate([h, h, l, l], axis=0)


def near_sums(info, split, values, lhs, acc, near_count):
    per_device = (info.shape[0] - 1) // 2
    leaf_size = split.shape[2]
    acc[...] = jnp.zeros_like(acc)
    step = STEP

    def visit(n, carry):
        for a in range(per_device):
            slot = info[a, n]
            right = quad(split[slot])
            w = values[slot]
            for r in range(leaf_size // step):
                at = a * leaf_size + r * step
                e = jnp.exp2(dot(lhs[at : at + step, :], right))
                e = e.reshape(step // 8, 8, leaf_size) * w[None]
                acc[at : at + step, :] += fold(e.reshape(step, leaf_size))
        return carry

    lax.fori_loop(0, near_count, visit, 0, unroll=UNROLL)


def far_sums(info, far_blocks, vec, far_count, subs, per_side, offset):
    per_device = (info.shape[0] - 1) // 2
    skel_count = far_blocks.shape[1]
    outs = []
    for a in range(per_device):
        total = jnp.zeros((skel_count, LANES), F32)
        for n in range(far_count):
            slot = info[per_device + a, n]
            w = picked_row(vec, info, slot, per_side, subs, offset, skel_count)
            total = total + far_blocks[a * far_count + n] * w
        outs.append(jnp.sum(total, axis=1, keepdims=True))
    return outs


def top_sums(top, vec, subs, offset):
    leaf_count, skel_count, _ = top.shape
    total = jnp.zeros((skel_count, LANES), F32)
    for u in range(leaf_count):
        w = jnp.sum(vec[u * subs : (u + 1) * subs, offset : offset + skel_count], axis=0, keepdims=True)
        total = total + top[u] * w
    return jnp.sum(total, axis=1, keepdims=True)


def gathered(acc, u_row, uz_col, lm, rm, v_row, skel_out, root_out):
    per_device, skel_count, leaf_size = lm.shape
    outs = []
    for a in range(per_device):
        part = slice(a * leaf_size, (a + 1) * leaf_size)
        y = row_sums(acc[part, :]) * u_row[:, part]
        col = skel_out[a] * uz_col[a * skel_count : (a + 1) * skel_count, :1]
        y = y + jnp.sum(lm[a] * col + rm[a] * root_out, axis=0, keepdims=True)
        outs.append(y + RIDGE * v_row[:, part])
    return jnp.concatenate(outs, axis=1)


def first_kernel(
    counts, info, ritz, window, lhs, z_lhs, u_row, uz_row, uz_col, lm, rm, top, v_row, vec,
    first_row, sent, split, far_blocks, landed, values, acc, sems,
):
    near_count, far_count = counts
    per_device, skel_count, leaf_size = lm.shape
    subs, sides, feats, count = window.shape
    per_side = subs * per_device
    copies = [pltpu.make_async_copy(window.at[d], landed.at[d], sems.at[d]) for d in range(subs)]
    for copy in copies:
        copy.start()
    spread_values(info, vec, values, subs, leaf_size)
    skel_at = count + per_device * skel_count
    root_out = top_sums(top, vec, subs, skel_at)
    for d in range(subs):
        copies[d].wait()
        for side in range(sides):
            for j in range(per_device):
                h, l = halves(landed[d, side, :, j * leaf_size : (j + 1) * leaf_size])
                slot = side * per_side + d * per_device + j
                split[slot, :feats, :] = h
                split[slot, feats:, :] = l
    near_sums(info, split, values, lhs, acc, near_count)
    index_at = skel_at + skel_count
    for a in range(per_device):
        for n in range(far_count):
            slot = info[per_device + a, n]
            index = picked_row(vec, info, slot, per_side, subs, index_at, skel_count).astype(jnp.int32)
            hot = pick(index, leaf_size).astype(F32).astype(BF16)
            z = dot(split[slot], hot).astype(BF16)
            left = z_lhs[a * skel_count : (a + 1) * skel_count, :]
            far_blocks[a * far_count + n] = jnp.exp2(dot(left, quad(z)))
    skel_out = far_sums(info, far_blocks, vec, far_count, subs, per_side, count)
    y = gathered(acc, u_row, uz_col, lm, rm, v_row, skel_out, root_out)
    first = v_row[...] - y / ritz[0]
    first_row[...] = first
    block = jnp.concatenate(packed_vector(first, u_row, uz_row, lm, rm), axis=1)
    sent[...] = jnp.broadcast_to(block, sent.shape)


def second_kernel(
    counts, info, ritz, lhs, u_row, uz_col, lm, rm, top, split, far_blocks, v_row, vec, tree_row, order,
    sent, values, acc,
):
    near_count, far_count = counts
    per_device, skel_count, leaf_size = lm.shape
    subs, count = sent.shape
    spread_values(info, vec, values, subs, leaf_size)
    root_out = top_sums(top, vec, subs, count + per_device * skel_count)
    skel_out = far_sums(info, far_blocks, vec, far_count, subs, subs * per_device, count)
    near_sums(info, split, values, lhs, acc, near_count)
    y = gathered(acc, u_row, uz_col, lm, rm, v_row, skel_out, root_out)
    grown = tree_row[...] - (v_row[...] - y / ritz[1])
    tiles = count // LANES
    row, lane = split_order(order[...])
    spread = jnp.where(pick(row, subs * tiles), grown, 0.0)
    hot = pick(lane, LANES).astype(F32).astype(BF16)
    placed = sum(dot(part, hot, NT) for part in thirds(spread))
    for k in range(tiles):
        sent[:, k * LANES : (k + 1) * LANES] = placed[k * subs : (k + 1) * subs]


def project_kernel(got, basis, user_row, sent):
    user = jnp.sum(got[...], axis=0, keepdims=True)
    user_row[...] = user
    b = basis[...]
    vecs = b.shape[0]
    proj = jnp.sum(b * user, axis=1, keepdims=True)
    norm = jnp.sum(user * user, axis=1, keepdims=True)
    lane = lax.broadcasted_iota(jnp.int32, (vecs, LANES), 1)
    sub = lax.broadcasted_iota(jnp.int32, (vecs, LANES), 0)
    row = jnp.sum(jnp.where(lane == sub, proj, 0.0), axis=0, keepdims=True)
    row = row + jnp.where(lane[:1] == vecs, norm, 0.0)
    sent[...] = jnp.broadcast_to(row, sent.shape)


def finish_kernel(got, tab, basis, user_row, orth, hess):
    b = basis[...]
    vecs = b.shape[0]
    total = jnp.sum(got[...], axis=0, keepdims=True)
    width = tab.shape[1]
    gram = jnp.sum(tab[:, width - LANES :], axis=0, keepdims=True)
    lane = lax.broadcasted_iota(jnp.int32, (vecs, LANES), 1)
    sub = lax.broadcasted_iota(jnp.int32, (vecs, LANES), 0)
    proj = jnp.sum(jnp.where(lane == sub, total, 0.0), axis=1, keepdims=True)
    left = jnp.sum(jnp.where(lane // vecs == sub, proj, 0.0), axis=0, keepdims=True)
    right = jnp.sum(jnp.where((lane & (vecs - 1)) == sub, proj, 0.0), axis=0, keepdims=True)
    one = lane[:1]
    norm = jnp.sum(jnp.where(one == vecs, total, 0.0), axis=1, keepdims=True)
    cross = jnp.sum(jnp.where(one < vecs, total * total, 0.0), axis=1, keepdims=True)
    quad = jnp.sum(left * right * gram, axis=1, keepdims=True)
    length = jnp.sqrt(jnp.maximum(norm - 2.0 * cross + quad, 0.0) + EPSILON)
    orth[...] = user_row[...] - jnp.sum(proj * b, axis=0, keepdims=True)
    hess[...] = jnp.where(one < vecs, total, jnp.broadcast_to(length, (1, LANES)))


def shards(
    points,
    leaf_maps,
    root_maps,
    current,
    krylov_basis,
    ritz_roots,
    point_order,
    skeleton,
    root_skeleton,
    near_list,
    far_list,
):
    per_device, skel_count, leaf_size = leaf_maps.shape
    count, feats = points.shape
    vecs = krylov_basis.shape[0]
    subs = lax.axis_size("sub")
    leaves = lax.axis_size("leaf")
    everyone = subs * leaves
    me = lax.axis_index("leaf")
    scale = math.sqrt(math.log2(math.e) / (feats / 2.0))
    qt = points.T * F32(scale)
    ring = [(i, (i + 1) % leaves) for i in range(leaves)]
    back = [(j, i) for i, j in ring]
    low = lax.ppermute(qt, "leaf", ring)
    high = lax.ppermute(qt, "leaf", back)
    window = lax.all_gather(jnp.stack([low, qt, high]), "sub", axis=0)

    sds = jax.ShapeDtypeStruct
    near_count, far_count = near_list.shape[1], far_list.shape[1]
    info = jnp.concatenate(
        [
            near_list,
            jnp.pad(far_list, ((0, 0), (0, near_count - far_count))),
            jnp.full((1, near_count), me, jnp.int32),
        ],
        axis=0,
    )
    order = point_order.reshape(1, count)
    rskel = root_skeleton - lax.axis_index("sub") * count

    lhs, u_row, z_lhs, uz_row, uz_col, sent, gram = call(
        functools.partial(prepare_kernel, scale, leaf_size),
        [
            sds((count, 4 * feats), BF16),
            sds((1, count), F32),
            sds((per_device * skel_count, 4 * feats), BF16),
            sds((per_device, skel_count), F32),
            sds((per_device * skel_count, LANES), F32),
            sds((subs, count + (feats // subs) * skel_count), F32),
            sds((1, LANES), F32),
        ],
        points,
        qt,
        skeleton,
        rskel,
        current.reshape(1, count),
        krylov_basis,
        name="prepare",
    )
    got = lax.all_to_all(sent, "sub", 0, 0, tiled=True)
    vec_width = count + per_device * skel_count + skel_count
    tab_width = vec_width + per_device * skel_count + (feats // subs) * skel_count + LANES
    tree_row, sent = call(
        start_kernel,
        [sds((1, count), F32), sds((everyone, tab_width), F32)],
        got,
        order,
        u_row,
        uz_row,
        leaf_maps,
        root_maps,
        skeleton,
        gram,
        name="start",
    )
    tab = lax.all_to_all(sent, BOTH, 0, 0, tiled=True)
    (top,) = call(
        functools.partial(top_kernel, feats),
        [sds((leaves, skel_count, skel_count), F32)],
        info,
        tab,
        smem=(0,),
        name="top",
    )
    slots = 3 * subs * per_device
    counts = (near_count, far_count)
    spread = pltpu.VMEM((slots, 8, leaf_size), F32)
    sums = pltpu.VMEM((count, LANES), F32)
    first_row, sent, split, far_blocks = call(
        functools.partial(first_kernel, counts),
        [
            sds((1, count), F32),
            sds((everyone, vec_width), F32),
            sds((slots, 2 * feats, leaf_size), BF16),
            sds((per_device * far_count, skel_count, skel_count), F32),
        ],
        info,
        ritz_roots,
        window,
        lhs,
        z_lhs,
        u_row,
        uz_row,
        uz_col,
        leaf_maps,
        root_maps,
        top,
        tree_row,
        tab,
        smem=(0, 1),
        far=(2,),
        scratch=[pltpu.VMEM(window.shape, F32), spread, sums, pltpu.SemaphoreType.DMA((subs,))],
        name="first",
    )
    vec = lax.all_to_all(sent, BOTH, 0, 0, tiled=True)
    (sent,) = call(
        functools.partial(second_kernel, counts),
        [sds((subs, count), F32)],
        info,
        ritz_roots,
        lhs,
        u_row,
        uz_col,
        leaf_maps,
        root_maps,
        top,
        split,
        far_blocks,
        first_row,
        vec,
        tree_row,
        order,
        smem=(0, 1),
        scratch=[spread, sums],
        name="second",
    )
    got = lax.all_to_all(sent, "sub", 0, 0, tiled=True)
    user_row, sent = call(
        project_kernel,
        [sds((1, count), F32), sds((everyone, LANES), F32)],
        got,
        krylov_basis,
        name="project",
    )
    got = lax.all_to_all(sent, BOTH, 0, 0, tiled=True)
    orth, hess = call(
        finish_kernel,
        [sds((1, count), F32), sds((1, LANES), F32)],
        got,
        tab,
        krylov_basis,
        user_row,
        name="finish",
    )
    return orth.reshape(count), hess[0, : vecs + 1]


def solution(mesh):
    return jax.shard_map(
        shards,
        mesh=mesh,
        in_specs=(
            P(("leaf", "sub"), None),
            P(("leaf", "sub"), None, None),
            P(("leaf", "sub"), None, None),
            P(("leaf", "sub")),
            P(None, ("leaf", "sub")),
            P(),
            P(("leaf", "sub")),
            P(("leaf", "sub"), None),
            P("leaf", None),
            P(("leaf", "sub"), None),
            P(("leaf", "sub"), None),
        ),
        out_specs=(P(("leaf", "sub")), P()),
        check_vma=False,
    )
```

```python
import functools
import math

import jax
import jax.numpy as jnp
from jax import lax
from jax.experimental import pallas as pl
from jax.experimental.pallas import tpu as pltpu
from jax.sharding import PartitionSpec as P

F32 = jnp.float32
BF16 = jnp.bfloat16
HI = lax.Precision.HIGHEST
RIDGE = 1.0
EPSILON = 1e-06
LANES = 128
BOTH = ("leaf", "sub")
STEP = 256
UNROLL = 8
MIB = 1024 * 1024
NT = (((1,), (1,)), ((), ()))
TN = (((0,), (0,)), ((), ()))


def dot(a, b, dims=(((1,), (0,)), ((), ())), precision=None):
    return lax.dot_general(a, b, dims, precision=precision, preferred_element_type=F32)


def halves(x):
    h = x.astype(BF16)
    return h, (x - h.astype(F32)).astype(BF16)


def thirds(x):
    a = x.astype(BF16)
    r = x - a.astype(F32)
    b = r.astype(BF16)
    return a, b, (r - b.astype(F32)).astype(BF16)


def row_sums(block):
    return jnp.sum(block.T, axis=0, keepdims=True)


def fold(wide):
    return sum(wide[:, at : at + LANES] for at in range(0, wide.shape[1], LANES))


def half_norm(h, l):
    x = h.astype(F32) + l.astype(F32)
    return jnp.exp2(-0.5 * jnp.sum(x * x, axis=0, keepdims=True))


def pick(index_row, count):
    shape = (count, index_row.shape[1])
    return lax.broadcasted_iota(jnp.int32, shape, 0) == jnp.broadcast_to(index_row, shape)


def split_order(order):
    row = (lax.shift_right_logical(order, 7) & 7) * 8 + lax.shift_right_logical(order, 10)
    return row, order & 127


def call(body, outs, *args, smem=(), far=(), hbm_outs=(), scratch=(), cost=None, name=None, room=6):
    places = [pltpu.SMEM if i in smem else pl.ANY if i in far else pltpu.VMEM for i in range(len(args))]
    specs = [pl.BlockSpec(memory_space=place) for place in places]
    return pl.pallas_call(
        body,
        out_shape=outs,
        in_specs=specs,
        out_specs=[
            pl.BlockSpec(memory_space=pl.ANY if i in hbm_outs else pltpu.VMEM) for i in range(len(outs))
        ],
        scratch_shapes=list(scratch),
        compiler_params=pltpu.CompilerParams(vmem_limit_bytes=room * MIB),
        cost_estimate=cost,
        name=name,
    )(*args)


def prepare_kernel(
    scale, leaf_size, pts, qt, skel, rskel, cur, basis, lhs, u_row, z_lhs, uz_row, uz_col, sent, gram
):
    per_device, skel_count = skel.shape
    feats, count = qt.shape
    ph, pl_ = halves(pts[...] * scale)
    lhs[...] = jnp.concatenate([ph, pl_, ph, pl_], axis=1)
    qh, ql = halves(qt[...])
    u_row[...] = half_norm(qh, ql)
    both = jnp.concatenate([qh, ql], axis=0)
    for a in range(per_device):
        hot = pick(skel[a : a + 1, :], leaf_size).astype(F32).astype(BF16)
        z = dot(both[:, a * leaf_size : (a + 1) * leaf_size], hot)
        zh, zl = z[:feats].astype(BF16), z[feats:].astype(BF16)
        uz_row[a : a + 1, :] = half_norm(zh, zl)
        turned = z.T
        out = slice(a * skel_count, (a + 1) * skel_count)
        z_lhs[out, :] = jnp.concatenate([turned, turned], axis=1).astype(BF16)
        whole = turned[:, :feats] + turned[:, feats:]
        norm = jnp.exp2(-0.5 * jnp.sum(whole * whole, axis=1, keepdims=True))
        uz_col[out, :] = jnp.broadcast_to(norm, (skel_count, LANES))
    hot = pick(rskel[...], count).astype(F32).astype(BF16)
    r = dot(both, hot)
    r = r[:feats] + r[feats:]
    subs = sent.shape[0]
    sent[:, :count] = jnp.broadcast_to(cur[...], (subs, count))
    for f in range(feats // subs):
        sent[:, count + f * LANES : count + (f + 1) * LANES] = r[f * subs : (f + 1) * subs]
    g = dot(basis[...], basis[...], NT, HI)
    vecs = basis.shape[0]
    lane = lax.broadcasted_iota(jnp.int32, (vecs, LANES), 1)
    sub = lax.broadcasted_iota(jnp.int32, (vecs, LANES), 0)
    wide = dot(g, ((lane & (vecs - 1)) == sub).astype(F32), precision=HI)
    gram[...] = jnp.sum(jnp.where(lane // vecs == sub, wide, 0.0), axis=0, keepdims=True)


def packed_vector(v, u_row, uz_row, lm, rm):
    per_device, _, leaf_size = lm.shape
    root = None
    skel = []
    for a in range(per_device):
        piece = v[:, a * leaf_size : (a + 1) * leaf_size]
        skel.append(row_sums(fold(lm[a] * piece)) * uz_row[a : a + 1, :])
        part = fold(rm[a] * piece)
        root = part if root is None else root + part
    return [v * u_row[...]] + skel + [row_sums(root)]


def start_kernel(got, order, u_row, uz_row, lm, rm, skel, v_row, sent):
    subs = got.shape[0]
    count = order.shape[1]
    tiles = count // LANES
    cur = jnp.concatenate([got[:, k * LANES : (k + 1) * LANES] for k in range(tiles)], axis=0)
    row, lane = split_order(order[...])
    hot = pick(row, subs * tiles).astype(F32).astype(BF16)
    picked = sum(dot(part, hot, TN) for part in thirds(cur))
    v = jnp.sum(jnp.where(pick(lane, LANES), picked, 0.0), axis=0, keepdims=True)
    v_row[...] = v
    sums = []
    for k in range(tiles):
        at = count + k * LANES
        sums.append(jnp.sum(got[:, at : at + LANES], axis=0, keepdims=True))
    skels = [skel[a : a + 1, :].astype(F32) for a in range(skel.shape[0])]
    block = jnp.concatenate(
        packed_vector(v, u_row, uz_row, lm, rm) + skels + sums, axis=1
    )
    sent[...] = block


def top_kernel(feats, info, tab, blocks):
    leaf_count, skel_count, _ = blocks.shape
    subs = tab.shape[0] // leaf_count
    at = tab.shape[1] - feats // subs * skel_count
    me = info[info.shape[0] - 1, 0]

    def root_points(u):
        rows = pl.ds(pl.multiple_of(u * subs, subs), subs)
        tiles = [tab[rows, at + f * skel_count : at + (f + 1) * skel_count] for f in range(feats // subs)]
        return jnp.concatenate(tiles, axis=0)

    turned = root_points(me).T
    th, tl = halves(turned)
    left = jnp.concatenate([th, tl, th, tl], axis=1)
    whole = th.astype(F32) + tl.astype(F32)
    own = jnp.exp2(-0.5 * jnp.sum(whole * whole, axis=1, keepdims=True))

    def subtree(u, carry):
        h, l = halves(root_points(u))
        e = jnp.exp2(dot(left, jnp.concatenate([h, h, l, l], axis=0)))
        side = jnp.where(u == me, 0.0, half_norm(h, l))
        blocks[u] = e * side * own
        return carry

    lax.fori_loop(0, leaf_count, subtree, 0, unroll=2)


def owners(info, leaf_count, sides):
    me = info[info.shape[0] - 1, 0]
    return [(me + side + leaf_count - 1) % leaf_count for side in range(sides)]


def spread_values(info, vec, values, subs, leaf_size):
    slots = values.shape[0]
    leaf_count = vec.shape[0] // subs
    per_side = slots // 3
    for side, owner in enumerate(owners(info, leaf_count, 3)):
        block = vec[pl.ds(pl.multiple_of(owner * subs, subs), subs), : per_side // subs * leaf_size]
        for n in range(per_side):
            dev, j = n // (per_side // subs), n % (per_side // subs)
            row = block[dev : dev + 1, j * leaf_size : (j + 1) * leaf_size]
            values[side * per_side + n] = jnp.broadcast_to(row, (8, leaf_size))


def picked_row(ref, info, slot, per_side, subs, offset, size):
    leaf_count = ref.shape[0] // subs
    me = info[info.shape[0] - 1, 0]
    per_device = per_side // subs
    side, n = slot // per_side, slot % per_side
    owner = (me + side + leaf_count - 1) % leaf_count
    rows = pl.ds(pl.multiple_of(owner * subs, subs), subs)
    block = ref[rows, offset : offset + per_device * size]
    sub = lax.broadcasted_iota(jnp.int32, (subs, size), 0)
    out = jnp.zeros((1, size), F32)
    for j in range(per_device):
        mine = (sub == n // per_device) & (n % per_device == j)
        part = block[:, j * size : (j + 1) * size]
        out = out + jnp.sum(jnp.where(mine, part, 0.0), axis=0, keepdims=True)
    return out


def quad(pair):
    feats = pair.shape[0] // 2
    h, l = pair[:feats, :], pair[feats:, :]
    return jnp.concatenate([h, h, l, l], axis=0)


def near_sums(info, split, values, lhs, acc, near_count):
    per_device = (info.shape[0] - 1) // 2
    leaf_size = split.shape[2]
    acc[...] = jnp.zeros_like(acc)
    step = STEP

    def visit(n, carry):
        for a in range(per_device):
            slot = info[a, n]
            right = quad(split[slot])
            w = values[slot]
            for r in range(leaf_size // step):
                at = a * leaf_size + r * step
                e = jnp.exp2(dot(lhs[at : at + step, :], right))
                e = e.reshape(step // 8, 8, leaf_size) * w[None]
                acc[at : at + step, :] += fold(e.reshape(step, leaf_size))
        return carry

    lax.fori_loop(0, near_count, visit, 0, unroll=UNROLL)


def far_sums(info, far_blocks, vec, far_count, subs, per_side, offset):
    per_device = (info.shape[0] - 1) // 2
    skel_count = far_blocks.shape[1]
    outs = []
    for a in range(per_device):
        total = jnp.zeros((skel_count, LANES), F32)
        for n in range(far_count):
            slot = info[per_device + a, n]
            w = picked_row(vec, info, slot, per_side, subs, offset, skel_count)
            total = total + far_blocks[a * far_count + n] * w
        outs.append(jnp.sum(total, axis=1, keepdims=True))
    return outs


def top_sums(top, vec, subs, offset):
    leaf_count, skel_count, _ = top.shape
    total = jnp.zeros((skel_count, LANES), F32)
    for u in range(leaf_count):
        w = jnp.sum(vec[u * subs : (u + 1) * subs, offset : offset + skel_count], axis=0, keepdims=True)
        total = total + top[u] * w
    return jnp.sum(total, axis=1, keepdims=True)


def gathered(acc, u_row, uz_col, lm, rm, v_row, skel_out, root_out):
    per_device, skel_count, leaf_size = lm.shape
    outs = []
    for a in range(per_device):
        part = slice(a * leaf_size, (a + 1) * leaf_size)
        y = row_sums(acc[part, :]) * u_row[:, part]
        col = skel_out[a] * uz_col[a * skel_count : (a + 1) * skel_count, :1]
        y = y + jnp.sum(lm[a] * col + rm[a] * root_out, axis=0, keepdims=True)
        outs.append(y + RIDGE * v_row[:, part])
    return jnp.concatenate(outs, axis=1)


def first_kernel(
    counts, info, ritz, window, lhs, z_lhs, u_row, uz_row, uz_col, lm, rm, top, v_row, vec,
    first_row, sent, split_out, far_blocks, landed, split, values, acc, sems, out_sem,
):
    near_count, far_count = counts
    per_device, skel_count, leaf_size = lm.shape
    subs, sides, feats, count = window.shape
    per_side = subs * per_device
    copies = [pltpu.make_async_copy(window.at[d], landed.at[d], sems.at[d]) for d in range(subs)]
    for copy in copies:
        copy.start()
    spread_values(info, vec, values, subs, leaf_size)
    skel_at = count + per_device * skel_count
    root_out = top_sums(top, vec, subs, skel_at)
    for d in range(subs):
        copies[d].wait()
        for side in range(sides):
            for j in range(per_device):
                h, l = halves(landed[d, side, :, j * leaf_size : (j + 1) * leaf_size])
                slot = side * per_side + d * per_device + j
                split[slot, :feats, :] = h
                split[slot, feats:, :] = l
    written = pltpu.make_async_copy(split, split_out, out_sem)
    written.start()
    near_sums(info, split, values, lhs, acc, near_count)
    index_at = skel_at + skel_count
    for a in range(per_device):
        for n in range(far_count):
            slot = info[per_device + a, n]
            index = picked_row(vec, info, slot, per_side, subs, index_at, skel_count).astype(jnp.int32)
            hot = pick(index, leaf_size).astype(F32).astype(BF16)
            z = dot(split[slot], hot).astype(BF16)
            left = z_lhs[a * skel_count : (a + 1) * skel_count, :]
            far_blocks[a * far_count + n] = jnp.exp2(dot(left, quad(z)))
    skel_out = far_sums(info, far_blocks, vec, far_count, subs, per_side, count)
    y = gathered(acc, u_row, uz_col, lm, rm, v_row, skel_out, root_out)
    first = v_row[...] - y / ritz[0]
    first_row[...] = first
    written.wait()
    block = jnp.concatenate(packed_vector(first, u_row, uz_row, lm, rm), axis=1)
    sent[...] = block


def second_kernel(
    counts, info, ritz, lhs, u_row, uz_col, lm, rm, top, split_in, far_blocks, v_row, vec, tree_row, order,
    sent, values, acc, split, sems,
):
    near_count, far_count = counts
    per_device, skel_count, leaf_size = lm.shape
    subs, count = sent.shape
    read = pltpu.make_async_copy(split_in, split, sems)
    read.start()
    spread_values(info, vec, values, subs, leaf_size)
    root_out = top_sums(top, vec, subs, count + per_device * skel_count)
    skel_out = far_sums(info, far_blocks, vec, far_count, subs, subs * per_device, count)
    read.wait()
    near_sums(info, split, values, lhs, acc, near_count)
    y = gathered(acc, u_row, uz_col, lm, rm, v_row, skel_out, root_out)
    grown = tree_row[...] - (v_row[...] - y / ritz[1])
    tiles = count // LANES
    row, lane = split_order(order[...])
    spread = jnp.where(pick(row, subs * tiles), grown, 0.0)
    hot = pick(lane, LANES).astype(F32).astype(BF16)
    placed = sum(dot(part, hot, NT) for part in thirds(spread))
    for k in range(tiles):
        sent[:, k * LANES : (k + 1) * LANES] = placed[k * subs : (k + 1) * subs]


def project_kernel(got, basis, gram, user_row, sent):
    user = jnp.sum(got[...], axis=0, keepdims=True)
    user_row[...] = user
    b = basis[...]
    vecs = b.shape[0]
    proj = jnp.sum(b * user, axis=1, keepdims=True)
    norm = jnp.sum(user * user, axis=1, keepdims=True)
    lane = lax.broadcasted_iota(jnp.int32, (vecs, LANES), 1)
    sub = lax.broadcasted_iota(jnp.int32, (vecs, LANES), 0)
    row = jnp.sum(jnp.where(lane == sub, proj, 0.0), axis=0, keepdims=True)
    row = row + jnp.where(lane[:1] == vecs, norm, 0.0)
    sent[...] = jnp.concatenate([row, gram[...]], axis=1)


def finish_kernel(got, basis, user_row, orth, hess):
    b = basis[...]
    vecs = b.shape[0]
    total = jnp.sum(got[...], axis=0, keepdims=True)
    total, gram = total[:, :LANES], total[:, LANES:]
    lane = lax.broadcasted_iota(jnp.int32, (vecs, LANES), 1)
    sub = lax.broadcasted_iota(jnp.int32, (vecs, LANES), 0)
    proj = jnp.sum(jnp.where(lane == sub, total, 0.0), axis=1, keepdims=True)
    left = jnp.sum(jnp.where(lane // vecs == sub, proj, 0.0), axis=0, keepdims=True)
    right = jnp.sum(jnp.where((lane & (vecs - 1)) == sub, proj, 0.0), axis=0, keepdims=True)
    one = lane[:1]
    norm = jnp.sum(jnp.where(one == vecs, total, 0.0), axis=1, keepdims=True)
    cross = jnp.sum(jnp.where(one < vecs, total * total, 0.0), axis=1, keepdims=True)
    quad = jnp.sum(left * right * gram, axis=1, keepdims=True)
    length = jnp.sqrt(jnp.maximum(norm - 2.0 * cross + quad, 0.0) + EPSILON)
    orth[...] = user_row[...] - jnp.sum(proj * b, axis=0, keepdims=True)
    hess[...] = jnp.where(one < vecs, total, jnp.broadcast_to(length, (1, LANES)))


def to_all(row, everyone):
    return lax.all_to_all(jnp.broadcast_to(row, (everyone, row.shape[1])), BOTH, 0, 0, tiled=True)


def shards(
    points,
    leaf_maps,
    root_maps,
    current,
    krylov_basis,
    ritz_roots,
    point_order,
    skeleton,
    root_skeleton,
    near_list,
    far_list,
):
    per_device, skel_count, leaf_size = leaf_maps.shape
    count, feats = points.shape
    vecs = krylov_basis.shape[0]
    subs = lax.axis_size("sub")
    leaves = lax.axis_size("leaf")
    everyone = subs * leaves
    me = lax.axis_index("leaf")
    scale = math.sqrt(math.log2(math.e) / (feats / 2.0))
    qt = points.T * F32(scale)
    ring = [(i, (i + 1) % leaves) for i in range(leaves)]
    back = [(j, i) for i, j in ring]
    low = lax.ppermute(qt, "leaf", ring)
    high = lax.ppermute(qt, "leaf", back)
    window = lax.all_gather(jnp.stack([low, qt, high]), "sub", axis=0)

    sds = jax.ShapeDtypeStruct
    near_count, far_count = near_list.shape[1], far_list.shape[1]
    info = jnp.concatenate(
        [
            near_list,
            jnp.pad(far_list, ((0, 0), (0, near_count - far_count))),
            jnp.full((1, near_count), me, jnp.int32),
        ],
        axis=0,
    )
    order = point_order.reshape(1, count)
    rskel = root_skeleton - lax.axis_index("sub") * count

    lhs, u_row, z_lhs, uz_row, uz_col, sent, gram = call(
        functools.partial(prepare_kernel, scale, leaf_size),
        [
            sds((count, 4 * feats), BF16),
            sds((1, count), F32),
            sds((per_device * skel_count, 4 * feats), BF16),
            sds((per_device, skel_count), F32),
            sds((per_device * skel_count, LANES), F32),
            sds((subs, count + (feats // subs) * skel_count), F32),
            sds((1, LANES), F32),
        ],
        points,
        qt,
        skeleton,
        rskel,
        current.reshape(1, count),
        krylov_basis,
        name="prepare",
    )
    got = lax.all_to_all(sent, "sub", 0, 0, tiled=True)
    vec_width = count + per_device * skel_count + skel_count
    tab_width = vec_width + per_device * skel_count + (feats // subs) * skel_count
    tree_row, sent = call(
        start_kernel,
        [sds((1, count), F32), sds((1, tab_width), F32)],
        got,
        order,
        u_row,
        uz_row,
        leaf_maps,
        root_maps,
        skeleton,
        name="start",
    )
    tab = to_all(sent, everyone)
    (top,) = call(
        functools.partial(top_kernel, feats),
        [sds((leaves, skel_count, skel_count), F32)],
        info,
        tab,
        smem=(0,),
        name="top",
    )
    slots = 3 * subs * per_device
    counts = (near_count, far_count)
    spread = pltpu.VMEM((slots, 8, leaf_size), F32)
    sums = pltpu.VMEM((count, LANES), F32)
    halved = pltpu.VMEM((slots, 2 * feats, leaf_size), BF16)
    first_row, sent, split, far_blocks = call(
        functools.partial(first_kernel, counts),
        [
            sds((1, count), F32),
            sds((1, vec_width), F32),
            sds((slots, 2 * feats, leaf_size), BF16),
            sds((per_device * far_count, skel_count, skel_count), F32),
        ],
        info,
        ritz_roots,
        window,
        lhs,
        z_lhs,
        u_row,
        uz_row,
        uz_col,
        leaf_maps,
        root_maps,
        top,
        tree_row,
        tab,
        smem=(0, 1),
        far=(2,),
        hbm_outs=(2,),
        scratch=[
            pltpu.VMEM(window.shape, F32),
            halved,
            spread,
            sums,
            pltpu.SemaphoreType.DMA((subs,)),
            pltpu.SemaphoreType.DMA,
        ],
        room=58,
        name="first",
    )
    vec = to_all(sent, everyone)
    (sent,) = call(
        functools.partial(second_kernel, counts),
        [sds((subs, count), F32)],
        info,
        ritz_roots,
        lhs,
        u_row,
        uz_col,
        leaf_maps,
        root_maps,
        top,
        split,
        far_blocks,
        first_row,
        vec,
        tree_row,
        order,
        smem=(0, 1),
        far=(8,),
        scratch=[spread, sums, halved, pltpu.SemaphoreType.DMA],
        room=58,
        name="second",
    )
    got = lax.all_to_all(sent, "sub", 0, 0, tiled=True)
    user_row, sent = call(
        project_kernel,
        [sds((1, count), F32), sds((1, 2 * LANES), F32)],
        got,
        krylov_basis,
        gram,
        name="project",
    )
    got = to_all(sent, everyone)
    orth, hess = call(
        finish_kernel,
        [sds((1, count), F32), sds((1, LANES), F32)],
        got,
        krylov_basis,
        user_row,
        name="finish",
    )
    return orth.reshape(count), hess[0, : vecs + 1]


def solution(mesh):
    return jax.shard_map(
        shards,
        mesh=mesh,
        in_specs=(
            P(("leaf", "sub"), None),
            P(("leaf", "sub"), None, None),
            P(("leaf", "sub"), None, None),
            P(("leaf", "sub")),
            P(None, ("leaf", "sub")),
            P(),
            P(("leaf", "sub")),
            P(("leaf", "sub"), None),
            P("leaf", None),
            P(("leaf", "sub"), None),
            P(("leaf", "sub"), None),
        ),
        out_specs=(P(("leaf", "sub")), P()),
        check_vma=False,
    )
```

```python
import functools
import math

import jax
import jax.numpy as jnp
from jax import lax
from jax.experimental import pallas as pl
from jax.experimental.pallas import tpu as pltpu
from jax.sharding import PartitionSpec as P

F32 = jnp.float32
BF16 = jnp.bfloat16
HI = lax.Precision.HIGHEST
RIDGE = 1.0
EPSILON = 1e-06
LANES = 128
BOTH = ("leaf", "sub")
STEP = 256
UNROLL = 8
MIB = 1024 * 1024
NT = (((1,), (1,)), ((), ()))
TN = (((0,), (0,)), ((), ()))


def dot(a, b, dims=(((1,), (0,)), ((), ())), precision=None):
    return lax.dot_general(a, b, dims, precision=precision, preferred_element_type=F32)


def halves(x):
    h = x.astype(BF16)
    return h, (x - h.astype(F32)).astype(BF16)


def thirds(x):
    a = x.astype(BF16)
    r = x - a.astype(F32)
    b = r.astype(BF16)
    return a, b, (r - b.astype(F32)).astype(BF16)


def row_sums(block):
    return jnp.sum(block.T, axis=0, keepdims=True)


def fold(wide):
    return sum(wide[:, at : at + LANES] for at in range(0, wide.shape[1], LANES))


def half_norm(h, l):
    x = h.astype(F32) + l.astype(F32)
    return jnp.exp2(-0.5 * jnp.sum(x * x, axis=0, keepdims=True))


def pick(index_row, count):
    shape = (count, index_row.shape[1])
    return lax.broadcasted_iota(jnp.int32, shape, 0) == jnp.broadcast_to(index_row, shape)


def split_order(order):
    row = (lax.shift_right_logical(order, 7) & 7) * 8 + lax.shift_right_logical(order, 10)
    return row, order & 127


def call(body, outs, *args, smem=(), far=(), hbm_outs=(), scratch=(), cost=None, name=None, room=50):
    places = [pltpu.SMEM if i in smem else pl.ANY if i in far else pltpu.VMEM for i in range(len(args))]
    specs = [pl.BlockSpec(memory_space=place) for place in places]
    return pl.pallas_call(
        body,
        out_shape=outs,
        in_specs=specs,
        out_specs=[
            pl.BlockSpec(memory_space=pl.ANY if i in hbm_outs else pltpu.VMEM) for i in range(len(outs))
        ],
        scratch_shapes=list(scratch),
        compiler_params=pltpu.CompilerParams(vmem_limit_bytes=room * MIB),
        cost_estimate=cost,
        name=name,
    )(*args)


def prepare_kernel(leaf_size, qt, skel, rskel, cur, u_row, z_lhs, uz_row, uz_col, sent):
    per_device, skel_count = skel.shape
    feats, count = qt.shape
    qh, ql = halves(qt[...])
    u_row[...] = half_norm(qh, ql)
    both = jnp.concatenate([qh, ql], axis=0)
    for a in range(per_device):
        hot = pick(skel[a : a + 1, :], leaf_size).astype(F32).astype(BF16)
        z = dot(both[:, a * leaf_size : (a + 1) * leaf_size], hot)
        zh, zl = z[:feats].astype(BF16), z[feats:].astype(BF16)
        uz_row[a : a + 1, :] = half_norm(zh, zl)
        turned = z.T
        out = slice(a * skel_count, (a + 1) * skel_count)
        z_lhs[out, :] = jnp.concatenate([turned, turned], axis=1).astype(BF16)
        whole = turned[:, :feats] + turned[:, feats:]
        norm = jnp.exp2(-0.5 * jnp.sum(whole * whole, axis=1, keepdims=True))
        uz_col[out, :] = jnp.broadcast_to(norm, (skel_count, LANES))
    hot = pick(rskel[...], count).astype(F32).astype(BF16)
    r = dot(both, hot)
    r = r[:feats] + r[feats:]
    subs = sent.shape[0]
    sent[:, :count] = jnp.broadcast_to(cur[...], (subs, count))
    for f in range(feats // subs):
        sent[:, count + f * LANES : count + (f + 1) * LANES] = r[f * subs : (f + 1) * subs]


def own_kernel(scale, pts, basis, lhs, gram):
    ph, pl_ = halves(pts[...] * scale)
    lhs[...] = jnp.concatenate([ph, pl_, ph, pl_], axis=1)
    g = dot(basis[...], basis[...], NT, HI)
    vecs = basis.shape[0]
    lane = lax.broadcasted_iota(jnp.int32, (vecs, LANES), 1)
    sub = lax.broadcasted_iota(jnp.int32, (vecs, LANES), 0)
    wide = dot(g, ((lane & (vecs - 1)) == sub).astype(F32), precision=HI)
    first = LANES - vecs * vecs
    gram[...] = jnp.sum(jnp.where((lane - first) // vecs == sub, wide, 0.0), axis=0, keepdims=True)


def packed_vector(v, u_row, uz_row, lm, rm):
    per_device, _, leaf_size = lm.shape
    root = None
    skel = []
    for a in range(per_device):
        piece = v[:, a * leaf_size : (a + 1) * leaf_size]
        skel.append(row_sums(fold(lm[a] * piece)) * uz_row[a : a + 1, :])
        part = fold(rm[a] * piece)
        root = part if root is None else root + part
    return [v * u_row[...]] + skel + [row_sums(root)]


def start_kernel(got, order, u_row, uz_row, lm, rm, skel, v_row, near_sent, far_sent):
    subs = got.shape[0]
    count = order.shape[1]
    tiles = count // LANES
    cur = jnp.concatenate([got[:, k * LANES : (k + 1) * LANES] for k in range(tiles)], axis=0)
    row, lane = split_order(order[...])
    hot = pick(row, subs * tiles).astype(F32).astype(BF16)
    picked = sum(dot(part, hot, TN) for part in thirds(cur))
    v = jnp.sum(jnp.where(pick(lane, LANES), picked, 0.0), axis=0, keepdims=True)
    v_row[...] = v
    sums = []
    for k in range(tiles):
        at = count + k * LANES
        sums.append(jnp.sum(got[:, at : at + LANES], axis=0, keepdims=True))
    skels = [skel[a : a + 1, :].astype(F32) for a in range(skel.shape[0])]
    *near, root = packed_vector(v, u_row, uz_row, lm, rm)
    near_sent[...] = jnp.concatenate(near + skels, axis=1)
    far_sent[...] = jnp.concatenate([root] + sums, axis=1)


def top_kernel(feats, info, tab, blocks):
    leaf_count, skel_count, _ = blocks.shape
    subs = tab.shape[0] // leaf_count
    at = tab.shape[1] - feats // subs * skel_count
    me = info[info.shape[0] - 1, 0]

    def root_points(u):
        rows = pl.ds(pl.multiple_of(u * subs, subs), subs)
        tiles = [tab[rows, at + f * skel_count : at + (f + 1) * skel_count] for f in range(feats // subs)]
        return jnp.concatenate(tiles, axis=0)

    turned = root_points(me).T
    th, tl = halves(turned)
    left = jnp.concatenate([th, tl, th, tl], axis=1)
    whole = th.astype(F32) + tl.astype(F32)
    own = jnp.exp2(-0.5 * jnp.sum(whole * whole, axis=1, keepdims=True))

    def subtree(u, carry):
        h, l = halves(root_points(u))
        e = jnp.exp2(dot(left, jnp.concatenate([h, h, l, l], axis=0)))
        side = jnp.where(u == me, 0.0, half_norm(h, l))
        blocks[u] = e * side * own
        return carry

    lax.fori_loop(0, leaf_count, subtree, 0, unroll=2)


def side_blocks(info, vec, subs, sides, start, stop):
    leaf_count = vec.shape[0] // subs
    me = info[info.shape[0] - 1, 0]
    blocks = []
    for side in range(sides):
        owner = (me + side + leaf_count - 1) % leaf_count
        blocks.append(vec[pl.ds(pl.multiple_of(owner * subs, subs), subs), start:stop])
    return blocks


def spread_values(blocks, values):
    leaf_size = values.shape[2]
    subs, count = blocks[0].shape
    slot = 0
    for block in blocks:
        for dev in range(subs):
            for at in range(0, count, leaf_size):
                row = block[dev : dev + 1, at : at + leaf_size]
                values[slot] = jnp.broadcast_to(row, (8, leaf_size))
                slot += 1


def picked_row(blocks, slot, size):
    subs, width = blocks[0].shape
    per_device = width // size
    sub = lax.broadcasted_iota(jnp.int32, (subs, size), 0)
    out = jnp.zeros((subs, size), F32)
    for side, block in enumerate(blocks):
        for j in range(per_device):
            mine = (side * subs + sub) * per_device + j == slot
            out = jnp.where(mine, block[:, j * size : (j + 1) * size], out)
    return jnp.sum(out, axis=0, keepdims=True)


def quad(pair):
    feats = pair.shape[0] // 2
    h, l = pair[:feats, :], pair[feats:, :]
    return jnp.concatenate([h, h, l, l], axis=0)


def near_sums(info, split, values, lhs, acc, near_count):
    per_device = (info.shape[0] - 1) // 2
    leaf_size = split.shape[2]
    acc[...] = jnp.zeros_like(acc)
    step = STEP

    def visit(n, carry):
        for a in range(per_device):
            slot = info[a, n]
            right = quad(split[slot])
            w = values[slot]
            for r in range(leaf_size // step):
                at = a * leaf_size + r * step
                e = jnp.exp2(dot(lhs[at : at + step, :], right))
                e = e.reshape(step // 8, 8, leaf_size) * w[None]
                acc[at : at + step, :] += fold(e.reshape(step, leaf_size))
        return carry

    lax.fori_loop(0, near_count, visit, 0, unroll=UNROLL)


def far_sums(info, far_blocks, blocks, far_count):
    per_device = (info.shape[0] - 1) // 2
    skel_count = far_blocks.shape[1]
    outs = []
    for a in range(per_device):
        total = jnp.zeros((skel_count, LANES), F32)
        for n in range(far_count):
            w = picked_row(blocks, info[per_device + a, n], skel_count)
            total = total + far_blocks[a * far_count + n] * w
        outs.append(jnp.sum(total, axis=1, keepdims=True))
    return outs


def top_sums(top, vec, subs, offset):
    leaf_count, skel_count, _ = top.shape
    total = jnp.zeros((skel_count, LANES), F32)
    for u in range(leaf_count):
        w = jnp.sum(vec[u * subs : (u + 1) * subs, offset : offset + skel_count], axis=0, keepdims=True)
        total = total + top[u] * w
    return jnp.sum(total, axis=1, keepdims=True)


def gathered(acc, u_row, uz_col, lm, rm, v_row, skel_out, root_out):
    per_device, skel_count, leaf_size = lm.shape
    outs = []
    for a in range(per_device):
        part = slice(a * leaf_size, (a + 1) * leaf_size)
        y = row_sums(acc[part, :]) * u_row[:, part]
        col = skel_out[a] * uz_col[a * skel_count : (a + 1) * skel_count, :1]
        y = y + jnp.sum(lm[a] * col + rm[a] * root_out, axis=0, keepdims=True)
        outs.append(y + RIDGE * v_row[:, part])
    return jnp.concatenate(outs, axis=1)


def first_kernel(
    counts, info, ritz, window, lhs, z_lhs, u_row, uz_row, uz_col, lm, rm, top, v_row, vec, tab,
    first_row, sent, split_out, far_blocks, landed, split, values, acc, sems, out_sem,
):
    near_count, far_count = counts
    per_device, skel_count, leaf_size = lm.shape
    subs, sides, feats, count = window.shape
    per_side = subs * per_device
    copies = [pltpu.make_async_copy(window.at[d], landed.at[d], sems.at[d]) for d in range(subs)]
    for copy in copies:
        copy.start()
    width = vec.shape[1] // sides
    skels = per_device * skel_count

    def sides_of(start, size):
        return [vec[:, side * width + start : side * width + start + size] for side in range(sides)]

    spread_values(sides_of(0, count), values)
    root_out = top_sums(top, tab, subs, 0)
    for d in range(subs):
        copies[d].wait()
        for side in range(sides):
            for j in range(per_device):
                h, l = halves(landed[d, side, :, j * leaf_size : (j + 1) * leaf_size])
                slot = side * per_side + d * per_device + j
                split[slot, :feats, :] = h
                split[slot, feats:, :] = l
    written = pltpu.make_async_copy(split, split_out, out_sem)
    written.start()
    near_sums(info, split, values, lhs, acc, near_count)
    indices = sides_of(count + skels, skels)
    for a in range(per_device):
        for n in range(far_count):
            slot = info[per_device + a, n]
            hot = pick(picked_row(indices, slot, skel_count).astype(jnp.int32), leaf_size)
            z = dot(split[slot], hot.astype(F32).astype(BF16)).astype(BF16)
            left = z_lhs[a * skel_count : (a + 1) * skel_count, :]
            far_blocks[a * far_count + n] = jnp.exp2(dot(left, quad(z)))
    skel_out = far_sums(info, far_blocks, sides_of(count, skels), far_count)
    y = gathered(acc, u_row, uz_col, lm, rm, v_row, skel_out, root_out)
    first = v_row[...] - y / ritz[0]
    first_row[...] = first
    written.wait()
    block = jnp.concatenate(packed_vector(first, u_row, uz_row, lm, rm), axis=1)
    sent[...] = block


def second_kernel(
    counts, info, ritz, lhs, u_row, uz_col, lm, rm, top, split, far_blocks, v_row, vec, tree_row, order,
    sent, values, acc,
):
    near_count, far_count = counts
    per_device, skel_count, leaf_size = lm.shape
    subs, count = sent.shape
    sides = values.shape[0] // (subs * per_device)
    skels = per_device * skel_count
    spread_values(side_blocks(info, vec, subs, sides, 0, count), values)
    root_out = top_sums(top, vec, subs, count + skels)
    far_weights = side_blocks(info, vec, subs, sides, count, count + skels)
    skel_out = far_sums(info, far_blocks, far_weights, far_count)
    near_sums(info, split, values, lhs, acc, near_count)
    y = gathered(acc, u_row, uz_col, lm, rm, v_row, skel_out, root_out)
    grown = tree_row[...] - (v_row[...] - y / ritz[1])
    tiles = count // LANES
    row, lane = split_order(order[...])
    spread = jnp.where(pick(row, subs * tiles), grown, 0.0)
    hot = pick(lane, LANES).astype(F32).astype(BF16)
    placed = sum(dot(part, hot, NT) for part in thirds(spread))
    for k in range(tiles):
        sent[:, k * LANES : (k + 1) * LANES] = placed[k * subs : (k + 1) * subs]


def project_kernel(got, basis, gram, user_row, sent):
    user = jnp.sum(got[...], axis=0, keepdims=True)
    user_row[...] = user
    b = basis[...]
    vecs = b.shape[0]
    proj = jnp.sum(b * user, axis=1, keepdims=True)
    norm = jnp.sum(user * user, axis=1, keepdims=True)
    lane = lax.broadcasted_iota(jnp.int32, (vecs, LANES), 1)
    sub = lax.broadcasted_iota(jnp.int32, (vecs, LANES), 0)
    row = jnp.sum(jnp.where(lane == sub, proj, 0.0), axis=0, keepdims=True)
    row = row + jnp.where(lane[:1] == vecs, norm, 0.0)
    sent[...] = row + gram[...]


def finish_kernel(got, basis, user_row, orth, hess):
    b = basis[...]
    vecs = b.shape[0]
    total = jnp.sum(got[...], axis=0, keepdims=True)
    lane = lax.broadcasted_iota(jnp.int32, (vecs, LANES), 1)
    sub = lax.broadcasted_iota(jnp.int32, (vecs, LANES), 0)
    proj = jnp.sum(jnp.where(lane == sub, total, 0.0), axis=1, keepdims=True)
    first = LANES - vecs * vecs
    left = jnp.sum(jnp.where((lane - first) // vecs == sub, proj, 0.0), axis=0, keepdims=True)
    right = jnp.sum(jnp.where((lane & (vecs - 1)) == sub, proj, 0.0), axis=0, keepdims=True)
    one = lane[:1]
    norm = jnp.sum(jnp.where(one == vecs, total, 0.0), axis=1, keepdims=True)
    cross = jnp.sum(jnp.where(one < vecs, total * total, 0.0), axis=1, keepdims=True)
    quad = jnp.sum(left * right * total, axis=1, keepdims=True)
    length = jnp.sqrt(jnp.maximum(norm - 2.0 * cross + quad, 0.0) + EPSILON)
    orth[...] = user_row[...] - jnp.sum(proj * b, axis=0, keepdims=True)
    hess[...] = jnp.where(one < vecs, total, jnp.broadcast_to(length, (1, LANES)))


def to_all(row, everyone):
    return lax.all_to_all(jnp.broadcast_to(row, (everyone, row.shape[1])), BOTH, 0, 0, tiled=True)


def shards(
    points,
    leaf_maps,
    root_maps,
    current,
    krylov_basis,
    ritz_roots,
    point_order,
    skeleton,
    root_skeleton,
    near_list,
    far_list,
):
    per_device, skel_count, leaf_size = leaf_maps.shape
    count, feats = points.shape
    vecs = krylov_basis.shape[0]
    subs = lax.axis_size("sub")
    leaves = lax.axis_size("leaf")
    everyone = subs * leaves
    me = lax.axis_index("leaf")
    scale = math.sqrt(math.log2(math.e) / (feats / 2.0))
    qt = points.T * F32(scale)
    ring = [(i, (i + 1) % leaves) for i in range(leaves)]
    back = [(j, i) for i, j in ring]
    low = lax.ppermute(qt, "leaf", ring)
    high = lax.ppermute(qt, "leaf", back)

    sds = jax.ShapeDtypeStruct
    near_count, far_count = near_list.shape[1], far_list.shape[1]
    info = jnp.concatenate(
        [
            near_list,
            jnp.pad(far_list, ((0, 0), (0, near_count - far_count))),
            jnp.full((1, near_count), me, jnp.int32),
        ],
        axis=0,
    )
    order = point_order.reshape(1, count)
    rskel = root_skeleton - lax.axis_index("sub") * count

    u_row, z_lhs, uz_row, uz_col, sent = call(
        functools.partial(prepare_kernel, leaf_size),
        [
            sds((1, count), F32),
            sds((per_device * skel_count, 4 * feats), BF16),
            sds((per_device, skel_count), F32),
            sds((per_device * skel_count, LANES), F32),
            sds((subs, count + (feats // subs) * skel_count), F32),
        ],
        qt,
        skeleton,
        rskel,
        current.reshape(1, count),
        name="prepare",
    )
    got = lax.all_to_all(sent, "sub", 0, 0, tiled=True)
    held, got = lax.optimization_barrier((jnp.stack([low, qt, high]), got))
    window = lax.all_gather(held, "sub", axis=0)
    lhs, gram = call(
        functools.partial(own_kernel, scale),
        [sds((count, 4 * feats), BF16), sds((1, LANES), F32)],
        points,
        krylov_basis,
        name="own",
    )
    vec_width = count + per_device * skel_count + skel_count
    skels = per_device * skel_count
    near_width = count + 2 * skels
    tree_row, near_row, far_row = call(
        start_kernel,
        [
            sds((1, count), F32),
            sds((1, near_width), F32),
            sds((1, skel_count * (1 + feats // subs)), F32),
        ],
        got,
        order,
        u_row,
        uz_row,
        leaf_maps,
        root_maps,
        skeleton,
        name="start",
    )
    near_row, tab = lax.optimization_barrier((near_row, to_all(far_row, everyone)))
    sides = [lax.ppermute(near_row, "leaf", ring), near_row, lax.ppermute(near_row, "leaf", back)]
    near_rows = jnp.concatenate(sides, axis=1)
    near_rows = jnp.broadcast_to(near_rows, (subs, near_rows.shape[1]))
    near_vec = lax.all_to_all(near_rows, "sub", 0, 0, tiled=True)
    (top,) = call(
        functools.partial(top_kernel, feats),
        [sds((leaves, skel_count, skel_count), F32)],
        info,
        tab,
        smem=(0,),
        name="top",
    )
    slots = 3 * subs * per_device
    counts = (near_count, far_count)
    spread = pltpu.VMEM((slots, 8, leaf_size), F32)
    sums = pltpu.VMEM((count, LANES), F32)
    halved = pltpu.VMEM((slots, 2 * feats, leaf_size), BF16)
    first_row, sent, split, far_blocks = call(
        functools.partial(first_kernel, counts),
        [
            sds((1, count), F32),
            sds((1, vec_width), F32),
            sds((slots, 2 * feats, leaf_size), BF16),
            sds((per_device * far_count, skel_count, skel_count), F32),
        ],
        info,
        ritz_roots,
        window,
        lhs,
        z_lhs,
        u_row,
        uz_row,
        uz_col,
        leaf_maps,
        root_maps,
        top,
        tree_row,
        near_vec,
        tab,
        smem=(0, 1),
        far=(2,),
        hbm_outs=(2,),
        scratch=[
            pltpu.VMEM(window.shape, F32),
            halved,
            spread,
            sums,
            pltpu.SemaphoreType.DMA((subs,)),
            pltpu.SemaphoreType.DMA,
        ],
        name="first",
    )
    vec = to_all(sent, everyone)
    (sent,) = call(
        functools.partial(second_kernel, counts),
        [sds((subs, count), F32)],
        info,
        ritz_roots,
        lhs,
        u_row,
        uz_col,
        leaf_maps,
        root_maps,
        top,
        split,
        far_blocks,
        first_row,
        vec,
        tree_row,
        order,
        smem=(0, 1),
        scratch=[spread, sums],
        name="second",
    )
    got = lax.all_to_all(sent, "sub", 0, 0, tiled=True)
    user_row, sent = call(
        project_kernel,
        [sds((1, count), F32), sds((1, LANES), F32)],
        got,
        krylov_basis,
        gram,
        name="project",
    )
    got = to_all(sent, everyone)
    orth, hess = call(
        finish_kernel,
        [sds((1, count), F32), sds((1, LANES), F32)],
        got,
        krylov_basis,
        user_row,
        name="finish",
    )
    return orth.reshape(count), hess[0, : vecs + 1]


def solution(mesh):
    return jax.shard_map(
        shards,
        mesh=mesh,
        in_specs=(
            P(("leaf", "sub"), None),
            P(("leaf", "sub"), None, None),
            P(("leaf", "sub"), None, None),
            P(("leaf", "sub")),
            P(None, ("leaf", "sub")),
            P(),
            P(("leaf", "sub")),
            P(("leaf", "sub"), None),
            P("leaf", None),
            P(("leaf", "sub"), None),
            P(("leaf", "sub"), None),
        ),
        out_specs=(P(("leaf", "sub")), P()),
        check_vma=False,
    )
```

```python
import functools
import math

import jax
import jax.numpy as jnp
from jax import lax
from jax.experimental import pallas as pl
from jax.experimental.pallas import tpu as pltpu
from jax.sharding import PartitionSpec as P

F32 = jnp.float32
BF16 = jnp.bfloat16
HI = lax.Precision.HIGHEST
RIDGE = 1.0
EPSILON = 1e-06
LANES = 128
BOTH = ("leaf", "sub")
STEP = 256
UNROLL = 8
MIB = 1024 * 1024
NT = (((1,), (1,)), ((), ()))
TN = (((0,), (0,)), ((), ()))


def dot(a, b, dims=(((1,), (0,)), ((), ())), precision=None):
    return lax.dot_general(a, b, dims, precision=precision, preferred_element_type=F32)


def halves(x):
    h = x.astype(BF16)
    return h, (x - h.astype(F32)).astype(BF16)


def thirds(x):
    a = x.astype(BF16)
    r = x - a.astype(F32)
    b = r.astype(BF16)
    return a, b, (r - b.astype(F32)).astype(BF16)


def row_sums(block):
    return jnp.sum(block.T, axis=0, keepdims=True)


def fold(wide):
    return sum(wide[:, at : at + LANES] for at in range(0, wide.shape[1], LANES))


def half_norm(h, l):
    x = h.astype(F32) + l.astype(F32)
    return jnp.exp2(-0.5 * jnp.sum(x * x, axis=0, keepdims=True))


def pick(index_row, count):
    shape = (count, index_row.shape[1])
    return lax.broadcasted_iota(jnp.int32, shape, 0) == jnp.broadcast_to(index_row, shape)


def split_order(order):
    row = (lax.shift_right_logical(order, 7) & 7) * 8 + lax.shift_right_logical(order, 10)
    return row, order & 127


def call(body, outs, *args, smem=(), far=(), hbm_outs=(), scratch=(), cost=None, name=None, room=50):
    places = [pltpu.SMEM if i in smem else pl.ANY if i in far else pltpu.VMEM for i in range(len(args))]
    specs = [pl.BlockSpec(memory_space=place) for place in places]
    return pl.pallas_call(
        body,
        out_shape=outs,
        in_specs=specs,
        out_specs=[
            pl.BlockSpec(memory_space=pl.ANY if i in hbm_outs else pltpu.VMEM) for i in range(len(outs))
        ],
        scratch_shapes=list(scratch),
        compiler_params=pltpu.CompilerParams(vmem_limit_bytes=room * MIB),
        cost_estimate=cost,
        name=name,
    )(*args)


def prepare_kernel(leaf_size, qt, skel, rskel, cur, u_row, z_lhs, uz_row, uz_col, sent):
    per_device, skel_count = skel.shape
    feats, count = qt.shape
    qh, ql = halves(qt[...])
    u_row[...] = half_norm(qh, ql)
    both = jnp.concatenate([qh, ql], axis=0)
    for a in range(per_device):
        hot = pick(skel[a : a + 1, :], leaf_size).astype(F32).astype(BF16)
        z = dot(both[:, a * leaf_size : (a + 1) * leaf_size], hot)
        zh, zl = z[:feats].astype(BF16), z[feats:].astype(BF16)
        uz_row[a : a + 1, :] = half_norm(zh, zl)
        turned = z.T
        out = slice(a * skel_count, (a + 1) * skel_count)
        z_lhs[out, :] = jnp.concatenate([turned, turned], axis=1).astype(BF16)
        whole = turned[:, :feats] + turned[:, feats:]
        norm = jnp.exp2(-0.5 * jnp.sum(whole * whole, axis=1, keepdims=True))
        uz_col[out, :] = jnp.broadcast_to(norm, (skel_count, LANES))
    hot = pick(rskel[...], count).astype(F32).astype(BF16)
    r = dot(both, hot)
    r = r[:feats] + r[feats:]
    subs = sent.shape[0]
    sent[:, :count] = jnp.broadcast_to(cur[...], (subs, count))
    for f in range(feats // subs):
        sent[:, count + f * LANES : count + (f + 1) * LANES] = r[f * subs : (f + 1) * subs]


def own_kernel(scale, pts, basis, lhs, gram):
    ph, pl_ = halves(pts[...] * scale)
    lhs[...] = jnp.concatenate([ph, pl_, ph, pl_], axis=1)
    g = dot(basis[...], basis[...], NT, HI)
    vecs = basis.shape[0]
    lane = lax.broadcasted_iota(jnp.int32, (vecs, LANES), 1)
    sub = lax.broadcasted_iota(jnp.int32, (vecs, LANES), 0)
    wide = dot(g, ((lane & (vecs - 1)) == sub).astype(F32), precision=HI)
    first = LANES - vecs * vecs
    gram[...] = jnp.sum(jnp.where((lane - first) // vecs == sub, wide, 0.0), axis=0, keepdims=True)


def packed_vector(v, u_row, uz_row, lm, rm):
    per_device, _, leaf_size = lm.shape
    root = None
    skel = []
    for a in range(per_device):
        piece = v[:, a * leaf_size : (a + 1) * leaf_size]
        skel.append(row_sums(fold(lm[a] * piece)) * uz_row[a : a + 1, :])
        part = fold(rm[a] * piece)
        root = part if root is None else root + part
    return [v * u_row[...]] + skel + [row_sums(root)]


def start_kernel(got, order, u_row, uz_row, lm, rm, skel, v_row, near_sent, far_sent):
    subs = got.shape[0]
    count = order.shape[1]
    tiles = count // LANES
    cur = jnp.concatenate([got[:, k * LANES : (k + 1) * LANES] for k in range(tiles)], axis=0)
    row, lane = split_order(order[...])
    hot = pick(row, subs * tiles).astype(F32).astype(BF16)
    picked = sum(dot(part, hot, TN) for part in thirds(cur))
    v = jnp.sum(jnp.where(pick(lane, LANES), picked, 0.0), axis=0, keepdims=True)
    v_row[...] = v
    sums = []
    for k in range(tiles):
        at = count + k * LANES
        sums.append(jnp.sum(got[:, at : at + LANES], axis=0, keepdims=True))
    skels = [skel[a : a + 1, :].astype(F32) for a in range(skel.shape[0])]
    *near, root = packed_vector(v, u_row, uz_row, lm, rm)
    near_sent[...] = jnp.concatenate(near + skels, axis=1)
    far_sent[...] = jnp.concatenate([root] + sums, axis=1)


def top_kernel(feats, info, tab, blocks):
    leaf_count, skel_count, _ = blocks.shape
    subs = tab.shape[0] // leaf_count
    at = tab.shape[1] - feats // subs * skel_count
    me = info[info.shape[0] - 1, 0]

    def root_points(u):
        rows = pl.ds(pl.multiple_of(u * subs, subs), subs)
        tiles = [tab[rows, at + f * skel_count : at + (f + 1) * skel_count] for f in range(feats // subs)]
        return jnp.concatenate(tiles, axis=0)

    turned = root_points(me).T
    th, tl = halves(turned)
    left = jnp.concatenate([th, tl, th, tl], axis=1)
    whole = th.astype(F32) + tl.astype(F32)
    own = jnp.exp2(-0.5 * jnp.sum(whole * whole, axis=1, keepdims=True))

    def subtree(u, carry):
        h, l = halves(root_points(u))
        e = jnp.exp2(dot(left, jnp.concatenate([h, h, l, l], axis=0)))
        side = jnp.where(u == me, 0.0, half_norm(h, l))
        blocks[u] = e * side * own
        return carry

    lax.fori_loop(0, leaf_count, subtree, 0, unroll=2)


def side_blocks(info, vec, subs, sides, start, stop):
    leaf_count = vec.shape[0] // subs
    me = info[info.shape[0] - 1, 0]
    blocks = []
    for side in range(sides):
        owner = (me + side + leaf_count - 1) % leaf_count
        blocks.append(vec[pl.ds(pl.multiple_of(owner * subs, subs), subs), start:stop])
    return blocks


def spread_values(blocks, values):
    leaf_size = values.shape[2]
    subs, count = blocks[0].shape
    slot = 0
    for block in blocks:
        for dev in range(subs):
            for at in range(0, count, leaf_size):
                row = block[dev : dev + 1, at : at + leaf_size]
                values[slot] = jnp.broadcast_to(row, (8, leaf_size))
                slot += 1


def picked_row(blocks, slot, size):
    subs, width = blocks[0].shape
    per_device = width // size
    sub = lax.broadcasted_iota(jnp.int32, (subs, size), 0)
    out = jnp.zeros((subs, size), F32)
    for side, block in enumerate(blocks):
        for j in range(per_device):
            mine = (side * subs + sub) * per_device + j == slot
            out = jnp.where(mine, block[:, j * size : (j + 1) * size], out)
    return jnp.sum(out, axis=0, keepdims=True)


def quad(pair):
    feats = pair.shape[0] // 2
    h, l = pair[:feats, :], pair[feats:, :]
    return jnp.concatenate([h, h, l, l], axis=0)


def near_sums(info, split, values, lhs, acc, near_count):
    per_device = (info.shape[0] - 1) // 2
    leaf_size = split.shape[2]
    acc[...] = jnp.zeros_like(acc)
    step = STEP

    def visit(n, carry):
        for a in range(per_device):
            slot = info[a, n]
            right = quad(split[slot])
            w = values[slot]
            for r in range(leaf_size // step):
                at = a * leaf_size + r * step
                e = jnp.exp2(dot(lhs[at : at + step, :], right))
                e = e.reshape(step // 8, 8, leaf_size) * w[None]
                acc[at : at + step, :] += fold(e.reshape(step, leaf_size))
        return carry

    lax.fori_loop(0, near_count, visit, 0, unroll=UNROLL)


def far_sums(info, far_blocks, blocks, far_count):
    per_device = (info.shape[0] - 1) // 2
    skel_count = far_blocks.shape[1]
    outs = []
    for a in range(per_device):
        total = jnp.zeros((skel_count, LANES), F32)
        for n in range(far_count):
            w = picked_row(blocks, info[per_device + a, n], skel_count)
            total = total + far_blocks[a * far_count + n] * w
        outs.append(jnp.sum(total, axis=1, keepdims=True))
    return outs


def top_sums(top, vec, subs, offset):
    leaf_count, skel_count, _ = top.shape
    total = jnp.zeros((skel_count, LANES), F32)
    for u in range(leaf_count):
        w = jnp.sum(vec[u * subs : (u + 1) * subs, offset : offset + skel_count], axis=0, keepdims=True)
        total = total + top[u] * w
    return jnp.sum(total, axis=1, keepdims=True)


def gathered(acc, u_row, uz_col, lm, rm, v_row, skel_out, root_out):
    per_device, skel_count, leaf_size = lm.shape
    outs = []
    for a in range(per_device):
        part = slice(a * leaf_size, (a + 1) * leaf_size)
        y = row_sums(acc[part, :]) * u_row[:, part]
        col = skel_out[a] * uz_col[a * skel_count : (a + 1) * skel_count, :1]
        y = y + jnp.sum(lm[a] * col + rm[a] * root_out, axis=0, keepdims=True)
        outs.append(y + RIDGE * v_row[:, part])
    return jnp.concatenate(outs, axis=1)


def bring(sources, targets, sems):
    copies = [
        pltpu.make_async_copy(src, dst, sems.at[n]) for n, (src, dst) in enumerate(zip(sources, targets))
    ]
    for copy in copies:
        copy.start()
    return copies


def first_kernel(
    counts, info, ritz, window, lhs, z_in, u_row, uz_row, uz_col, lm_in, rm_in, top_in, v_row, vec, tab_in,
    first_row, sent, split_out, far_blocks,
    landed, split, values, acc, z_lhs, lm, rm, top, tab, sems, late_sems, out_sem,
):
    near_count, far_count = counts
    per_device, skel_count, leaf_size = lm.shape
    subs, sides, feats, count = window.shape
    per_side = subs * per_device
    copies = [pltpu.make_async_copy(window.at[d], landed.at[d], sems.at[d]) for d in range(subs)]
    for copy in copies:
        copy.start()
    late = bring((z_in, top_in, tab_in, lm_in, rm_in), (z_lhs, top, tab, lm, rm), late_sems)
    width = vec.shape[1] // sides
    skels = per_device * skel_count

    def sides_of(start, size):
        return [vec[:, side * width + start : side * width + start + size] for side in range(sides)]

    spread_values(sides_of(0, count), values)
    for d in range(subs):
        copies[d].wait()
        for side in range(sides):
            for j in range(per_device):
                h, l = halves(landed[d, side, :, j * leaf_size : (j + 1) * leaf_size])
                slot = side * per_side + d * per_device + j
                split[slot, :feats, :] = h
                split[slot, feats:, :] = l
    written = pltpu.make_async_copy(split, split_out, out_sem)
    written.start()
    near_sums(info, split, values, lhs, acc, near_count)
    for copy in late:
        copy.wait()
    root_out = top_sums(top, tab, subs, 0)
    indices = sides_of(count + skels, skels)
    for a in range(per_device):
        for n in range(far_count):
            slot = info[per_device + a, n]
            hot = pick(picked_row(indices, slot, skel_count).astype(jnp.int32), leaf_size)
            z = dot(split[slot], hot.astype(F32).astype(BF16)).astype(BF16)
            left = z_lhs[a * skel_count : (a + 1) * skel_count, :]
            far_blocks[a * far_count + n] = jnp.exp2(dot(left, quad(z)))
    skel_out = far_sums(info, far_blocks, sides_of(count, skels), far_count)
    y = gathered(acc, u_row, uz_col, lm, rm, v_row, skel_out, root_out)
    first = v_row[...] - y / ritz[0]
    first_row[...] = first
    written.wait()
    block = jnp.concatenate(packed_vector(first, u_row, uz_row, lm, rm), axis=1)
    sent[...] = block


def second_kernel(
    counts, info, ritz, lhs, u_row, uz_col, lm, rm, top, split, far_blocks, v_row, vec, tree_row, order,
    sent, values, acc,
):
    near_count, far_count = counts
    per_device, skel_count, leaf_size = lm.shape
    subs, count = sent.shape
    sides = values.shape[0] // (subs * per_device)
    skels = per_device * skel_count
    spread_values(side_blocks(info, vec, subs, sides, 0, count), values)
    root_out = top_sums(top, vec, subs, count + skels)
    far_weights = side_blocks(info, vec, subs, sides, count, count + skels)
    skel_out = far_sums(info, far_blocks, far_weights, far_count)
    near_sums(info, split, values, lhs, acc, near_count)
    y = gathered(acc, u_row, uz_col, lm, rm, v_row, skel_out, root_out)
    grown = tree_row[...] - (v_row[...] - y / ritz[1])
    tiles = count // LANES
    row, lane = split_order(order[...])
    spread = jnp.where(pick(row, subs * tiles), grown, 0.0)
    hot = pick(lane, LANES).astype(F32).astype(BF16)
    placed = sum(dot(part, hot, NT) for part in thirds(spread))
    for k in range(tiles):
        sent[:, k * LANES : (k + 1) * LANES] = placed[k * subs : (k + 1) * subs]


def project_kernel(got, basis, gram, user_row, sent):
    user = jnp.sum(got[...], axis=0, keepdims=True)
    user_row[...] = user
    b = basis[...]
    vecs = b.shape[0]
    proj = jnp.sum(b * user, axis=1, keepdims=True)
    norm = jnp.sum(user * user, axis=1, keepdims=True)
    lane = lax.broadcasted_iota(jnp.int32, (vecs, LANES), 1)
    sub = lax.broadcasted_iota(jnp.int32, (vecs, LANES), 0)
    row = jnp.sum(jnp.where(lane == sub, proj, 0.0), axis=0, keepdims=True)
    row = row + jnp.where(lane[:1] == vecs, norm, 0.0)
    sent[...] = row + gram[...]


def finish_kernel(got, basis, user_row, orth, hess):
    b = basis[...]
    vecs = b.shape[0]
    total = jnp.sum(got[...], axis=0, keepdims=True)
    lane = lax.broadcasted_iota(jnp.int32, (vecs, LANES), 1)
    sub = lax.broadcasted_iota(jnp.int32, (vecs, LANES), 0)
    proj = jnp.sum(jnp.where(lane == sub, total, 0.0), axis=1, keepdims=True)
    first = LANES - vecs * vecs
    left = jnp.sum(jnp.where((lane - first) // vecs == sub, proj, 0.0), axis=0, keepdims=True)
    right = jnp.sum(jnp.where((lane & (vecs - 1)) == sub, proj, 0.0), axis=0, keepdims=True)
    one = lane[:1]
    norm = jnp.sum(jnp.where(one == vecs, total, 0.0), axis=1, keepdims=True)
    cross = jnp.sum(jnp.where(one < vecs, total * total, 0.0), axis=1, keepdims=True)
    quad = jnp.sum(left * right * total, axis=1, keepdims=True)
    length = jnp.sqrt(jnp.maximum(norm - 2.0 * cross + quad, 0.0) + EPSILON)
    orth[...] = user_row[...] - jnp.sum(proj * b, axis=0, keepdims=True)
    hess[...] = jnp.where(one < vecs, total, jnp.broadcast_to(length, (1, LANES)))


def to_all(row, everyone):
    return lax.all_to_all(jnp.broadcast_to(row, (everyone, row.shape[1])), BOTH, 0, 0, tiled=True)


def shards(
    points,
    leaf_maps,
    root_maps,
    current,
    krylov_basis,
    ritz_roots,
    point_order,
    skeleton,
    root_skeleton,
    near_list,
    far_list,
):
    per_device, skel_count, leaf_size = leaf_maps.shape
    count, feats = points.shape
    vecs = krylov_basis.shape[0]
    subs = lax.axis_size("sub")
    leaves = lax.axis_size("leaf")
    everyone = subs * leaves
    me = lax.axis_index("leaf")
    scale = math.sqrt(math.log2(math.e) / (feats / 2.0))
    qt = points.T * F32(scale)
    ring = [(i, (i + 1) % leaves) for i in range(leaves)]
    back = [(j, i) for i, j in ring]
    low = lax.ppermute(qt, "leaf", ring)
    high = lax.ppermute(qt, "leaf", back)

    sds = jax.ShapeDtypeStruct
    near_count, far_count = near_list.shape[1], far_list.shape[1]
    info = jnp.concatenate(
        [
            near_list,
            jnp.pad(far_list, ((0, 0), (0, near_count - far_count))),
            jnp.full((1, near_count), me, jnp.int32),
        ],
        axis=0,
    )
    order = point_order.reshape(1, count)
    rskel = root_skeleton - lax.axis_index("sub") * count

    u_row, z_lhs, uz_row, uz_col, sent = call(
        functools.partial(prepare_kernel, leaf_size),
        [
            sds((1, count), F32),
            sds((per_device * skel_count, 4 * feats), BF16),
            sds((per_device, skel_count), F32),
            sds((per_device * skel_count, LANES), F32),
            sds((subs, count + (feats // subs) * skel_count), F32),
        ],
        qt,
        skeleton,
        rskel,
        current.reshape(1, count),
        room=62,
        name="prepare",
    )
    got = lax.all_to_all(sent, "sub", 0, 0, tiled=True)
    held, got = lax.optimization_barrier((jnp.stack([low, qt, high]), got))
    window = lax.all_gather(held, "sub", axis=0)
    lhs, gram = call(
        functools.partial(own_kernel, scale),
        [sds((count, 4 * feats), BF16), sds((1, LANES), F32)],
        points,
        krylov_basis,
        name="own",
    )
    vec_width = count + per_device * skel_count + skel_count
    skels = per_device * skel_count
    near_width = count + 2 * skels
    tree_row, near_row, far_row = call(
        start_kernel,
        [
            sds((1, count), F32),
            sds((1, near_width), F32),
            sds((1, skel_count * (1 + feats // subs)), F32),
        ],
        got,
        order,
        u_row,
        uz_row,
        leaf_maps,
        root_maps,
        skeleton,
        room=62,
        name="start",
    )
    near_row, tab = lax.optimization_barrier((near_row, to_all(far_row, everyone)))
    sides = [lax.ppermute(near_row, "leaf", ring), near_row, lax.ppermute(near_row, "leaf", back)]
    near_rows = jnp.concatenate(sides, axis=1)
    near_rows = jnp.broadcast_to(near_rows, (subs, near_rows.shape[1]))
    near_vec = lax.all_to_all(near_rows, "sub", 0, 0, tiled=True)
    (top,) = call(
        functools.partial(top_kernel, feats),
        [sds((leaves, skel_count, skel_count), F32)],
        info,
        tab,
        smem=(0,),
        name="top",
    )
    slots = 3 * subs * per_device
    counts = (near_count, far_count)
    spread = pltpu.VMEM((slots, 8, leaf_size), F32)
    sums = pltpu.VMEM((count, LANES), F32)
    maps = pltpu.VMEM(leaf_maps.shape, F32)
    tops = pltpu.VMEM(top.shape, F32)
    halved = pltpu.VMEM((slots, 2 * feats, leaf_size), BF16)
    first_row, sent, split, far_blocks = call(
        functools.partial(first_kernel, counts),
        [
            sds((1, count), F32),
            sds((1, vec_width), F32),
            sds((slots, 2 * feats, leaf_size), BF16),
            sds((per_device * far_count, skel_count, skel_count), F32),
        ],
        info,
        ritz_roots,
        window,
        lhs,
        z_lhs,
        u_row,
        uz_row,
        uz_col,
        leaf_maps,
        root_maps,
        top,
        tree_row,
        near_vec,
        tab,
        smem=(0, 1),
        far=(2, 4, 8, 9, 10, 13),
        hbm_outs=(2,),
        scratch=[
            pltpu.VMEM(window.shape, F32),
            halved,
            spread,
            sums,
            pltpu.VMEM(z_lhs.shape, BF16),
            maps,
            maps,
            tops,
            pltpu.VMEM(tab.shape, F32),
            pltpu.SemaphoreType.DMA((subs,)),
            pltpu.SemaphoreType.DMA((5,)),
            pltpu.SemaphoreType.DMA,
        ],
        name="first",
    )
    vec = to_all(sent, everyone)
    (sent,) = call(
        functools.partial(second_kernel, counts),
        [sds((subs, count), F32)],
        info,
        ritz_roots,
        lhs,
        u_row,
        uz_col,
        leaf_maps,
        root_maps,
        top,
        split,
        far_blocks,
        first_row,
        vec,
        tree_row,
        order,
        smem=(0, 1),
        scratch=[spread, sums],
        name="second",
    )
    got = lax.all_to_all(sent, "sub", 0, 0, tiled=True)
    user_row, sent = call(
        project_kernel,
        [sds((1, count), F32), sds((1, LANES), F32)],
        got,
        krylov_basis,
        gram,
        name="project",
    )
    got = to_all(sent, everyone)
    orth, hess = call(
        finish_kernel,
        [sds((1, count), F32), sds((1, LANES), F32)],
        got,
        krylov_basis,
        user_row,
        name="finish",
    )
    return orth.reshape(count), hess[0, : vecs + 1]


def solution(mesh):
    return jax.shard_map(
        shards,
        mesh=mesh,
        in_specs=(
            P(("leaf", "sub"), None),
            P(("leaf", "sub"), None, None),
            P(("leaf", "sub"), None, None),
            P(("leaf", "sub")),
            P(None, ("leaf", "sub")),
            P(),
            P(("leaf", "sub")),
            P(("leaf", "sub"), None),
            P("leaf", None),
            P(("leaf", "sub"), None),
            P(("leaf", "sub"), None),
        ),
        out_specs=(P(("leaf", "sub")), P()),
        check_vma=False,
    )
```

```python
import functools
import math

import jax
import jax.numpy as jnp
from jax import lax
from jax.experimental import pallas as pl
from jax.experimental.pallas import tpu as pltpu
from jax.sharding import PartitionSpec as P

F32 = jnp.float32
BF16 = jnp.bfloat16
HI = lax.Precision.HIGHEST
RIDGE = 1.0
EPSILON = 1e-06
LANES = 128
BOTH = ("leaf", "sub")
STEP = 256
UNROLL = 8
MIB = 1024 * 1024
NT = (((1,), (1,)), ((), ()))
TN = (((0,), (0,)), ((), ()))


def dot(a, b, dims=(((1,), (0,)), ((), ())), precision=None):
    return lax.dot_general(a, b, dims, precision=precision, preferred_element_type=F32)


def halves(x):
    h = x.astype(BF16)
    return h, (x - h.astype(F32)).astype(BF16)


def thirds(x):
    a = x.astype(BF16)
    r = x - a.astype(F32)
    b = r.astype(BF16)
    return a, b, (r - b.astype(F32)).astype(BF16)


def row_sums(block):
    return jnp.sum(block.T, axis=0, keepdims=True)


def fold(wide):
    return sum(wide[:, at : at + LANES] for at in range(0, wide.shape[1], LANES))


def half_norm(h, l):
    x = h.astype(F32) + l.astype(F32)
    return jnp.exp2(-0.5 * jnp.sum(x * x, axis=0, keepdims=True))


def pick(index_row, count):
    shape = (count, index_row.shape[1])
    return lax.broadcasted_iota(jnp.int32, shape, 0) == jnp.broadcast_to(index_row, shape)


def split_order(order):
    row = (lax.shift_right_logical(order, 7) & 7) * 8 + lax.shift_right_logical(order, 10)
    return row, order & 127


def call(body, outs, *args, smem=(), far=(), hbm_outs=(), scratch=(), cost=None, name=None, room=50):
    places = [pltpu.SMEM if i in smem else pl.ANY if i in far else pltpu.VMEM for i in range(len(args))]
    specs = [pl.BlockSpec(memory_space=place) for place in places]
    return pl.pallas_call(
        body,
        out_shape=outs,
        in_specs=specs,
        out_specs=[
            pl.BlockSpec(memory_space=pl.ANY if i in hbm_outs else pltpu.VMEM) for i in range(len(outs))
        ],
        scratch_shapes=list(scratch),
        compiler_params=pltpu.CompilerParams(vmem_limit_bytes=room * MIB),
        cost_estimate=cost,
        name=name,
    )(*args)


def prepare_kernel(leaf_size, qt, skel, rskel, cur, u_row, z_lhs, uz_row, uz_col, sent):
    per_device, skel_count = skel.shape
    feats, count = qt.shape
    qh, ql = halves(qt[...])
    u_row[...] = half_norm(qh, ql)
    both = jnp.concatenate([qh, ql], axis=0)
    for a in range(per_device):
        hot = pick(skel[a : a + 1, :], leaf_size).astype(F32).astype(BF16)
        z = dot(both[:, a * leaf_size : (a + 1) * leaf_size], hot)
        zh, zl = z[:feats].astype(BF16), z[feats:].astype(BF16)
        uz_row[a : a + 1, :] = half_norm(zh, zl)
        turned = z.T
        out = slice(a * skel_count, (a + 1) * skel_count)
        z_lhs[out, :] = jnp.concatenate([turned, turned], axis=1).astype(BF16)
        whole = turned[:, :feats] + turned[:, feats:]
        norm = jnp.exp2(-0.5 * jnp.sum(whole * whole, axis=1, keepdims=True))
        uz_col[out, :] = jnp.broadcast_to(norm, (skel_count, LANES))
    hot = pick(rskel[...], count).astype(F32).astype(BF16)
    r = dot(both, hot)
    r = r[:feats] + r[feats:]
    subs = sent.shape[0]
    sent[:, :count] = jnp.broadcast_to(cur[...], (subs, count))
    for f in range(feats // subs):
        sent[:, count + f * LANES : count + (f + 1) * LANES] = r[f * subs : (f + 1) * subs]


def own_kernel(scale, pts, basis, lhs, gram):
    ph, pl_ = halves(pts[...] * scale)
    lhs[...] = jnp.concatenate([ph, pl_, ph, pl_], axis=1)
    g = dot(basis[...], basis[...], NT, HI)
    vecs = basis.shape[0]
    lane = lax.broadcasted_iota(jnp.int32, (vecs, LANES), 1)
    sub = lax.broadcasted_iota(jnp.int32, (vecs, LANES), 0)
    wide = dot(g, ((lane & (vecs - 1)) == sub).astype(F32), precision=HI)
    first = LANES - vecs * vecs
    gram[...] = jnp.sum(jnp.where((lane - first) // vecs == sub, wide, 0.0), axis=0, keepdims=True)


def packed_vector(v, u_row, uz_row, lm, rm):
    per_device, _, leaf_size = lm.shape
    root = None
    skel = []
    for a in range(per_device):
        piece = v[:, a * leaf_size : (a + 1) * leaf_size]
        skel.append(row_sums(fold(lm[a] * piece)) * uz_row[a : a + 1, :])
        part = fold(rm[a] * piece)
        root = part if root is None else root + part
    return [v * u_row[...]] + skel + [row_sums(root)]


def start_kernel(got, order, u_row, uz_row, lm, rm, skel, v_row, near_sent, far_sent):
    subs = got.shape[0]
    count = order.shape[1]
    tiles = count // LANES
    cur = jnp.concatenate([got[:, k * LANES : (k + 1) * LANES] for k in range(tiles)], axis=0)
    row, lane = split_order(order[...])
    hot = pick(row, subs * tiles).astype(F32).astype(BF16)
    picked = sum(dot(part, hot, TN) for part in thirds(cur))
    v = jnp.sum(jnp.where(pick(lane, LANES), picked, 0.0), axis=0, keepdims=True)
    v_row[...] = v
    sums = []
    for k in range(tiles):
        at = count + k * LANES
        sums.append(jnp.sum(got[:, at : at + LANES], axis=0, keepdims=True))
    skels = [skel[a : a + 1, :].astype(F32) for a in range(skel.shape[0])]
    *near, root = packed_vector(v, u_row, uz_row, lm, rm)
    near_sent[...] = jnp.concatenate(near + skels, axis=1)
    far_sent[...] = jnp.concatenate([root] + sums, axis=1)


def top_kernel(feats, info, tab, blocks):
    leaf_count, skel_count, _ = blocks.shape
    subs = tab.shape[0] // leaf_count
    at = tab.shape[1] - feats // subs * skel_count
    me = info[info.shape[0] - 1, 0]

    def root_points(u):
        rows = pl.ds(pl.multiple_of(u * subs, subs), subs)
        tiles = [tab[rows, at + f * skel_count : at + (f + 1) * skel_count] for f in range(feats // subs)]
        return jnp.concatenate(tiles, axis=0)

    turned = root_points(me).T
    th, tl = halves(turned)
    left = jnp.concatenate([th, tl, th, tl], axis=1)
    whole = th.astype(F32) + tl.astype(F32)
    own = jnp.exp2(-0.5 * jnp.sum(whole * whole, axis=1, keepdims=True))

    def subtree(u, carry):
        h, l = halves(root_points(u))
        e = jnp.exp2(dot(left, jnp.concatenate([h, h, l, l], axis=0)))
        side = jnp.where(u == me, 0.0, half_norm(h, l))
        blocks[u] = e * side * own
        return carry

    lax.fori_loop(0, leaf_count, subtree, 0, unroll=2)


def side_blocks(info, vec, subs, sides, start, stop):
    leaf_count = vec.shape[0] // subs
    me = info[info.shape[0] - 1, 0]
    blocks = []
    for side in range(sides):
        owner = (me + side + leaf_count - 1) % leaf_count
        blocks.append(vec[pl.ds(pl.multiple_of(owner * subs, subs), subs), start:stop])
    return blocks


def spread_values(blocks, values):
    leaf_size = values.shape[2]
    subs, count = blocks[0].shape
    slot = 0
    for block in blocks:
        for dev in range(subs):
            for at in range(0, count, leaf_size):
                row = block[dev : dev + 1, at : at + leaf_size]
                values[slot] = jnp.broadcast_to(row, (8, leaf_size))
                slot += 1


def picked_row(blocks, slot, size):
    subs, width = blocks[0].shape
    per_device = width // size
    sub = lax.broadcasted_iota(jnp.int32, (subs, size), 0)
    out = jnp.zeros((subs, size), F32)
    for side, block in enumerate(blocks):
        for j in range(per_device):
            mine = (side * subs + sub) * per_device + j == slot
            out = jnp.where(mine, block[:, j * size : (j + 1) * size], out)
    return jnp.sum(out, axis=0, keepdims=True)


def quad(pair):
    feats = pair.shape[0] // 2
    h, l = pair[:feats, :], pair[feats:, :]
    return jnp.concatenate([h, h, l, l], axis=0)


def near_sums(info, split, values, lhs, acc, near_count):
    per_device = (info.shape[0] - 1) // 2
    leaf_size = split.shape[2]
    acc[...] = jnp.zeros_like(acc)
    step = STEP

    def visit(n, carry):
        for a in range(per_device):
            slot = info[a, n]
            right = quad(split[slot])
            w = values[slot]
            for r in range(leaf_size // step):
                at = a * leaf_size + r * step
                e = jnp.exp2(dot(lhs[at : at + step, :], right))
                e = e.reshape(step // 8, 8, leaf_size) * w[None]
                acc[at : at + step, :] += fold(e.reshape(step, leaf_size))
        return carry

    lax.fori_loop(0, near_count, visit, 0, unroll=UNROLL)


def far_sums(info, far_blocks, blocks, far_count):
    per_device = (info.shape[0] - 1) // 2
    skel_count = far_blocks.shape[1]
    outs = []
    for a in range(per_device):
        total = jnp.zeros((skel_count, LANES), F32)
        for n in range(far_count):
            w = picked_row(blocks, info[per_device + a, n], skel_count)
            total = total + far_blocks[a * far_count + n] * w
        outs.append(jnp.sum(total, axis=1, keepdims=True))
    return outs


def top_sums(top, vec, subs, offset):
    leaf_count, skel_count, _ = top.shape
    total = jnp.zeros((skel_count, LANES), F32)
    for u in range(leaf_count):
        w = jnp.sum(vec[u * subs : (u + 1) * subs, offset : offset + skel_count], axis=0, keepdims=True)
        total = total + top[u] * w
    return jnp.sum(total, axis=1, keepdims=True)


def gathered(acc, u_row, uz_col, lm, rm, v_row, skel_out, root_out):
    per_device, skel_count, leaf_size = lm.shape
    outs = []
    for a in range(per_device):
        part = slice(a * leaf_size, (a + 1) * leaf_size)
        y = row_sums(acc[part, :]) * u_row[:, part]
        col = skel_out[a] * uz_col[a * skel_count : (a + 1) * skel_count, :1]
        y = y + jnp.sum(lm[a] * col + rm[a] * root_out, axis=0, keepdims=True)
        outs.append(y + RIDGE * v_row[:, part])
    return jnp.concatenate(outs, axis=1)


def bring(sources, targets, sems):
    copies = [
        pltpu.make_async_copy(src, dst, sems.at[n]) for n, (src, dst) in enumerate(zip(sources, targets))
    ]
    for copy in copies:
        copy.start()
    return copies


def first_kernel(
    counts, info, ritz, window, lhs, z_in, u_row, uz_row, uz_col, lm_in, rm_in, top_in, v_row, vec, tab_in,
    first_row, sent, split_out, far_blocks,
    landed, split, values, acc, z_lhs, lm, rm, top, tab, sems, late_sems, out_sem,
):
    near_count, far_count = counts
    per_device, skel_count, leaf_size = lm.shape
    subs, sides, feats, count = window.shape
    per_side = subs * per_device
    copies = [pltpu.make_async_copy(window.at[d], landed.at[d], sems.at[d]) for d in range(subs)]
    for copy in copies:
        copy.start()
    late = bring((z_in, top_in, tab_in, lm_in, rm_in), (z_lhs, top, tab, lm, rm), late_sems)
    width = vec.shape[1] // sides
    skels = per_device * skel_count

    def sides_of(start, size):
        return [vec[:, side * width + start : side * width + start + size] for side in range(sides)]

    spread_values(sides_of(0, count), values)
    for d in range(subs):
        copies[d].wait()
        for side in range(sides):
            for j in range(per_device):
                h, l = halves(landed[d, side, :, j * leaf_size : (j + 1) * leaf_size])
                slot = side * per_side + d * per_device + j
                split[slot, :feats, :] = h
                split[slot, feats:, :] = l
    written = pltpu.make_async_copy(split, split_out, out_sem)
    written.start()
    near_sums(info, split, values, lhs, acc, near_count)
    for copy in late:
        copy.wait()
    root_out = top_sums(top, tab, subs, 0)
    indices = sides_of(count + skels, skels)
    for a in range(per_device):
        for n in range(far_count):
            slot = info[per_device + a, n]
            hot = pick(picked_row(indices, slot, skel_count).astype(jnp.int32), leaf_size)
            z = dot(split[slot], hot.astype(F32).astype(BF16)).astype(BF16)
            left = z_lhs[a * skel_count : (a + 1) * skel_count, :]
            far_blocks[a * far_count + n] = jnp.exp2(dot(left, quad(z)))
    skel_out = far_sums(info, far_blocks, sides_of(count, skels), far_count)
    y = gathered(acc, u_row, uz_col, lm, rm, v_row, skel_out, root_out)
    first = v_row[...] - y / ritz[0]
    first_row[...] = first
    written.wait()
    block = jnp.concatenate(packed_vector(first, u_row, uz_row, lm, rm), axis=1)
    sent[...] = block


def second_kernel(
    counts, info, ritz, lhs, u_row, uz_col, lm, rm, top, split, far_blocks, v_row, vec, tree_row, order,
    sent, values, acc,
):
    near_count, far_count = counts
    per_device, skel_count, leaf_size = lm.shape
    subs, count = sent.shape
    sides = values.shape[0] // (subs * per_device)
    skels = per_device * skel_count
    spread_values(side_blocks(info, vec, subs, sides, 0, count), values)
    root_out = top_sums(top, vec, subs, count + skels)
    far_weights = side_blocks(info, vec, subs, sides, count, count + skels)
    skel_out = far_sums(info, far_blocks, far_weights, far_count)
    near_sums(info, split, values, lhs, acc, near_count)
    y = gathered(acc, u_row, uz_col, lm, rm, v_row, skel_out, root_out)
    grown = tree_row[...] - (v_row[...] - y / ritz[1])
    tiles = count // LANES
    row, lane = split_order(order[...])
    spread = jnp.where(pick(row, subs * tiles), grown, 0.0)
    hot = pick(lane, LANES).astype(F32).astype(BF16)
    placed = sum(dot(part, hot, NT) for part in thirds(spread))
    for k in range(tiles):
        sent[:, k * LANES : (k + 1) * LANES] = placed[k * subs : (k + 1) * subs]


def project_kernel(got, basis, gram, user_row, sent):
    user = jnp.sum(got[...], axis=0, keepdims=True)
    user_row[...] = user
    b = basis[...]
    vecs = b.shape[0]
    proj = jnp.sum(b * user, axis=1, keepdims=True)
    norm = jnp.sum(user * user, axis=1, keepdims=True)
    lane = lax.broadcasted_iota(jnp.int32, (vecs, LANES), 1)
    sub = lax.broadcasted_iota(jnp.int32, (vecs, LANES), 0)
    row = jnp.sum(jnp.where(lane == sub, proj, 0.0), axis=0, keepdims=True)
    row = row + jnp.where(lane[:1] == vecs, norm, 0.0)
    sent[...] = row + gram[...]


def finish_kernel(got, basis, user_row, orth, hess):
    b = basis[...]
    vecs = b.shape[0]
    total = jnp.sum(got[...], axis=0, keepdims=True)
    lane = lax.broadcasted_iota(jnp.int32, (vecs, LANES), 1)
    sub = lax.broadcasted_iota(jnp.int32, (vecs, LANES), 0)
    proj = jnp.sum(jnp.where(lane == sub, total, 0.0), axis=1, keepdims=True)
    first = LANES - vecs * vecs
    left = jnp.sum(jnp.where((lane - first) // vecs == sub, proj, 0.0), axis=0, keepdims=True)
    right = jnp.sum(jnp.where((lane & (vecs - 1)) == sub, proj, 0.0), axis=0, keepdims=True)
    one = lane[:1]
    norm = jnp.sum(jnp.where(one == vecs, total, 0.0), axis=1, keepdims=True)
    cross = jnp.sum(jnp.where(one < vecs, total * total, 0.0), axis=1, keepdims=True)
    quad = jnp.sum(left * right * total, axis=1, keepdims=True)
    length = jnp.sqrt(jnp.maximum(norm - 2.0 * cross + quad, 0.0) + EPSILON)
    orth[...] = user_row[...] - jnp.sum(proj * b, axis=0, keepdims=True)
    hess[...] = jnp.where(one < vecs, total, jnp.broadcast_to(length, (1, LANES)))


def to_all(row, everyone):
    return lax.all_to_all(jnp.broadcast_to(row, (everyone, row.shape[1])), BOTH, 0, 0, tiled=True)


def shards(
    points,
    leaf_maps,
    root_maps,
    current,
    krylov_basis,
    ritz_roots,
    point_order,
    skeleton,
    root_skeleton,
    near_list,
    far_list,
):
    per_device, skel_count, leaf_size = leaf_maps.shape
    count, feats = points.shape
    vecs = krylov_basis.shape[0]
    subs = lax.axis_size("sub")
    leaves = lax.axis_size("leaf")
    everyone = subs * leaves
    me = lax.axis_index("leaf")
    scale = math.sqrt(math.log2(math.e) / (feats / 2.0))
    qt = points.T * F32(scale)
    ring = [(i, (i + 1) % leaves) for i in range(leaves)]
    back = [(j, i) for i, j in ring]
    low = lax.ppermute(qt, "leaf", ring)
    high = lax.ppermute(qt, "leaf", back)

    sds = jax.ShapeDtypeStruct
    near_count, far_count = near_list.shape[1], far_list.shape[1]
    info = jnp.concatenate(
        [
            near_list,
            jnp.pad(far_list, ((0, 0), (0, near_count - far_count))),
            jnp.full((1, near_count), me, jnp.int32),
        ],
        axis=0,
    )
    order = point_order.reshape(1, count)
    rskel = root_skeleton - lax.axis_index("sub") * count

    u_row, z_lhs, uz_row, uz_col, sent = call(
        functools.partial(prepare_kernel, leaf_size),
        [
            sds((1, count), F32),
            sds((per_device * skel_count, 4 * feats), BF16),
            sds((per_device, skel_count), F32),
            sds((per_device * skel_count, LANES), F32),
            sds((subs, count + (feats // subs) * skel_count), F32),
        ],
        qt,
        skeleton,
        rskel,
        current.reshape(1, count),
        name="prepare",
    )
    got = lax.all_to_all(sent, "sub", 0, 0, tiled=True)
    held, got = lax.optimization_barrier((jnp.stack([low, qt, high]), got))
    window = lax.all_gather(held, "sub", axis=0)
    lhs, gram = call(
        functools.partial(own_kernel, scale),
        [sds((count, 4 * feats), BF16), sds((1, LANES), F32)],
        points,
        krylov_basis,
        name="own",
    )
    vec_width = count + per_device * skel_count + skel_count
    skels = per_device * skel_count
    near_width = count + 2 * skels
    tree_row, near_row, far_row = call(
        start_kernel,
        [
            sds((1, count), F32),
            sds((1, near_width), F32),
            sds((1, skel_count * (1 + feats // subs)), F32),
        ],
        got,
        order,
        u_row,
        uz_row,
        leaf_maps,
        root_maps,
        skeleton,
        name="start",
    )
    near_row, tab = lax.optimization_barrier((near_row, to_all(far_row, everyone)))
    sides = [lax.ppermute(near_row, "leaf", ring), near_row, lax.ppermute(near_row, "leaf", back)]
    near_rows = jnp.concatenate(sides, axis=1)
    near_rows = jnp.broadcast_to(near_rows, (subs, near_rows.shape[1]))
    near_vec = lax.all_to_all(near_rows, "sub", 0, 0, tiled=True)
    (top,) = call(
        functools.partial(top_kernel, feats),
        [sds((leaves, skel_count, skel_count), F32)],
        info,
        tab,
        smem=(0,),
        name="top",
    )
    slots = 3 * subs * per_device
    counts = (near_count, far_count)
    spread = pltpu.VMEM((slots, 8, leaf_size), F32)
    sums = pltpu.VMEM((count, LANES), F32)
    maps = pltpu.VMEM(leaf_maps.shape, F32)
    tops = pltpu.VMEM(top.shape, F32)
    halved = pltpu.VMEM((slots, 2 * feats, leaf_size), BF16)
    first_row, sent, split, far_blocks = call(
        functools.partial(first_kernel, counts),
        [
            sds((1, count), F32),
            sds((1, vec_width), F32),
            sds((slots, 2 * feats, leaf_size), BF16),
            sds((per_device * far_count, skel_count, skel_count), F32),
        ],
        info,
        ritz_roots,
        window,
        lhs,
        z_lhs,
        u_row,
        uz_row,
        uz_col,
        leaf_maps,
        root_maps,
        top,
        tree_row,
        near_vec,
        tab,
        smem=(0, 1),
        far=(2, 4, 8, 9, 10, 13),
        hbm_outs=(2,),
        scratch=[
            pltpu.VMEM(window.shape, F32),
            halved,
            spread,
            sums,
            pltpu.VMEM(z_lhs.shape, BF16),
            maps,
            maps,
            tops,
            pltpu.VMEM(tab.shape, F32),
            pltpu.SemaphoreType.DMA((subs,)),
            pltpu.SemaphoreType.DMA((5,)),
            pltpu.SemaphoreType.DMA,
        ],
        name="first",
    )
    vec = to_all(sent, everyone)
    (sent,) = call(
        functools.partial(second_kernel, counts),
        [sds((subs, count), F32)],
        info,
        ritz_roots,
        lhs,
        u_row,
        uz_col,
        leaf_maps,
        root_maps,
        top,
        split,
        far_blocks,
        first_row,
        vec,
        tree_row,
        order,
        smem=(0, 1),
        scratch=[spread, sums],
        name="second",
    )
    got = lax.all_to_all(sent, "sub", 0, 0, tiled=True)
    user_row, sent = call(
        project_kernel,
        [sds((1, count), F32), sds((1, LANES), F32)],
        got,
        krylov_basis,
        gram,
        name="project",
    )
    got = to_all(sent, everyone)
    orth, hess = call(
        finish_kernel,
        [sds((1, count), F32), sds((1, LANES), F32)],
        got,
        krylov_basis,
        user_row,
        name="finish",
    )
    return orth.reshape(count), hess[0, : vecs + 1]


def solution(mesh):
    return jax.shard_map(
        shards,
        mesh=mesh,
        in_specs=(
            P(("leaf", "sub"), None),
            P(("leaf", "sub"), None, None),
            P(("leaf", "sub"), None, None),
            P(("leaf", "sub")),
            P(None, ("leaf", "sub")),
            P(),
            P(("leaf", "sub")),
            P(("leaf", "sub"), None),
            P("leaf", None),
            P(("leaf", "sub"), None),
            P(("leaf", "sub"), None),
        ),
        out_specs=(P(("leaf", "sub")), P()),
        check_vma=False,
    )
```
